32 devices in a mesh: dom: 16 (over z, y, x), sub: 2 (over core).
Axes of the slice: x: 2, y: 2, z: 4, core: 2. Of those that a mesh axis runs over, the one named last changes fastest.
Arguments:
- voltages: float32 [64, 1024], P(None, ('dom', 'sub')), may hold values from -6 to 6
- newton_steps: float32 [2, 64, 1024], P(None, None, ('dom', 'sub')), may hold values from -3 to 3
- cap_diag: float32 [64, 1024], P(None, ('dom', 'sub')), may hold values from 1 to 10
- preconditioner: float32 [64, 64, 1024], P(None, None, ('dom', 'sub')), may hold values from -0.75 to 0.75
- couple_block: int32 [2048], P(('dom', 'sub')), may hold values from 0 to 31
- couple_owner: int32 [2048, 1], P(('dom', 'sub')), may hold values from 0 to 31; in each aligned block of 64 rows (0 to 63, 64 to 127, ...) at most 4 rows name the same one
- couple_offset: int32 [2048], P(('dom', 'sub')), may hold values from 0 to 31
- couple_source: int32 [2048, 768], P(('dom', 'sub')), may hold values from 0 to 63
- couple_target: int32 [2048, 768], P(('dom', 'sub')), may hold values from 0 to 63
- couple_gain: float32 [2048, 768], P(('dom', 'sub')), may hold values from 0.05 to 0.5
- inner_source: int32 [1024, 768], P(('dom', 'sub')), may hold values from 0 to 63
- inner_target: int32 [1024, 768], P(('dom', 'sub')), may hold values from 0 to 63
- inner_gain: float32 [1024, 768], P(('dom', 'sub')), may hold values from 0.05 to 0.5
Outputs:
- preconditioned: float32 [2, 64, 1024], P(None, None, ('dom', 'sub'))
The draws below stay inside these ranges and needn't reach their ends.
Inputs may be any that keep to these rules, and one draw needn't show every extreme that they name: `couple_owner`: within the 64 stamp blocks of one device no owner is named more than 4 times, a bound that some block reaches.
All inputs are finite; a program needn't handle non-finite values.
Results may differ from the reference program's by a relative error of at most 0.0041.
Values may be sent and summed in bfloat16 or wider, within the bound.
No kernel may reach another device: no remote copies, remote signals or barrier semaphores. Data moves between devices by JAX's collectives and lax.ppermute only.
A program may use at most 64 MiB of HBM per device.

```python
import math
import jax
import jax.numpy as jnp
import numpy as np
from jax import lax

BS = 64
BLK_DEV = 32
ST_DEV = 64
ELEM = 768
NEWTON = 2
CAP = 4
NBLK = 1024
STAMPS = 2048
N_DOM = 16
N_SUB = 2


def touch_ends(result, own_key, smallest, largest):
    shape = result.shape
    place = [jax.random.randint(jax.random.fold_in(own_key, axis), (), 0, shape[axis]) for axis in range(len(shape))]
    result = result.at[tuple(place)].set(smallest)
    longest = shape.index(max(shape))
    place[longest] = (place[longest] + 1) % shape[longest]
    return result.at[tuple(place)].set(largest)


def steps_of(stream_key, shape, cuts, least, top_value):
    def one(axis_at, shards_of):
        steps = jax.random.uniform(jax.random.fold_in(jax.random.fold_in(stream_key, 6), axis_at), (shards_of,), jnp.float32, least / len(cuts), top_value / len(cuts))
        return jnp.repeat(jnp.exp(steps), shape[axis_at] // shards_of).reshape((-1,) + (1,) * (len(shape) - axis_at - 1))

    level = one(*cuts[0])
    for cut in cuts[1:]:
        level = level * one(*cut)
    return level


def deal_out(rng, own, number, rows, amount, top, limit, skew):
    ranking = jax.random.permutation(rng, amount)
    packed, ordinary = load_shares(amount, rows * top, limit, skew, True), load_shares(amount, rows * top, limit, skew, False)
    places = jnp.arange(amount)

    def named(tallies, rotation):
        used = int((tallies > 0).sum())
        fixed = max(1, used // 4)
        moved = fixed + (places - fixed + rotation * (used - fixed)) % max(1, amount - fixed)
        return jnp.zeros((amount,), jnp.int32).at[ranking[jnp.where(places < fixed, places, moved)]].set(jnp.asarray(tallies, jnp.int32))

    tallies = jnp.where(number % 4 == 0, named(packed, number // 4), named(ordinary, number - number // 4 - 1))
    mixed = jax.random.permutation(jax.random.fold_in(own, 3), amount)
    source_of, taker = mixed[0:amount // 2 * 2:2], mixed[1:amount // 2 * 2:2]
    margin = jnp.minimum(tallies[source_of] - 1, limit - tallies[taker]) // 2
    margin = jnp.where((source_of == ranking[0]) | (taker == ranking[0]) | (tallies[taker] == 0), 0, jnp.maximum(margin, 0))
    moved = jax.random.randint(jax.random.fold_in(own, 4), (amount // 2,), 0, 1 << 20) % (margin + 1)
    tallies = tallies.at[source_of].add(-moved).at[taker].add(moved)
    labels = jnp.searchsorted(jnp.cumsum(tallies), jnp.arange(rows * top), side="right").astype(jnp.int32)
    listing = labels.reshape(top, rows).T
    listing = listing[jax.random.permutation(jax.random.fold_in(own, 1), rows)]
    rotation = jax.random.randint(jax.random.fold_in(own, 2), (rows, 1), 0, top)
    return jnp.take_along_axis(listing, (jnp.arange(top)[None, :] + rotation) % top, axis=1)


def load_shares(count, total, most, skew, full):
    portions = [(1 << 20) // math.isqrt(rank ** skew) + 1 for rank in range(1, count + 1)]
    largest = most if full else min(most, max(-(-total // count), total * portions[0] // sum(portions)))
    least = 1 if total - largest >= count - 1 else 0
    counts, rest = [largest] + [least] * (count - 1), total - largest - least * (count - 1)
    while rest > 0:
        movable = [i for i in range(1, count) if counts[i] < largest] or [i for i in range(1, count) if counts[i] < most]
        mass, remaining = sum([portions[i] for i in movable]), rest
        for i in movable:
            more = min(most - counts[i], max(1, remaining * portions[i] // mass), rest)
            counts[i] = counts[i] + more
            rest = rest - more
    return np.array(counts)


def noise(key, extent, deviation, limit, cuts=(), kind=jnp.bfloat16):
    drawn = deviation * jax.random.normal(key, extent, jnp.float32)
    if cuts:
        drawn = drawn * steps_of(key, extent, cuts, -0.22, 0.18)
    return jnp.clip(drawn, -limit, limit).astype(kind)


def setup_inputs(seed: int = 0) -> dict:
    key_list = jax.random.split(jax.random.key(seed), 14)
    voltages = noise(key_list[0], (BS, NBLK), 1.0, 6.0, ((1, 32),), jnp.float32)
    newton_steps = noise(key_list[1], (NEWTON, BS, NBLK), 0.5, 3.0, ((2, 32),), jnp.float32)
    cap_diag = jnp.clip(jnp.exp(math.log(10.0) - 2.3025851 * jax.random.uniform(key_list[2], (BS, NBLK), jnp.float32) ** steps_of(key_list[2], (BS, NBLK), ((1, 32),), -0.2, 0.2)), 1.0, 10.0)
    preconditioner = noise(key_list[3], (BS, BS, NBLK), BS ** -0.5, 0.75, ((2, 32),), jnp.float32)
    couple_block = touch_ends(jax.random.randint(key_list[4], (STAMPS,), 0, BLK_DEV), jax.random.fold_in(key_list[4], 1), 0, BLK_DEV - 1).astype(jnp.int32)
    couple_owner_keys = jax.random.split(jax.random.fold_in(key_list[5], 1), STAMPS // ST_DEV)
    couple_owner_turns = jax.random.permutation(jax.random.fold_in(key_list[5], 3), STAMPS // ST_DEV)
    couple_owner = jax.vmap(lambda own, number: deal_out(jax.random.fold_in(key_list[5], 2), own, number, ST_DEV, N_DOM * N_SUB, 1, CAP, 2))(couple_owner_keys, couple_owner_turns).reshape((STAMPS, 1))
    couple_offset = touch_ends(jax.random.randint(key_list[6], (STAMPS,), 0, BLK_DEV), jax.random.fold_in(key_list[6], 1), 0, BLK_DEV - 1).astype(jnp.int32)
    couple_source = touch_ends(jax.random.randint(key_list[7], (STAMPS, ELEM), 0, BS), jax.random.fold_in(key_list[7], 1), 0, BS - 1).astype(jnp.int32)
    couple_target = touch_ends(jax.random.randint(key_list[8], (STAMPS, ELEM), 0, BS), jax.random.fold_in(key_list[8], 1), 0, BS - 1).astype(jnp.int32)
    couple_gain = jnp.clip(jnp.exp(math.log(0.5) - 2.3025851 * jax.random.uniform(key_list[9], (STAMPS, ELEM), jnp.float32) ** steps_of(key_list[9], (STAMPS, ELEM), ((0, 32),), -0.2, 0.2)), 0.05, 0.5)
    inner_source = touch_ends(jax.random.randint(key_list[10], (NBLK, ELEM), 0, BS), jax.random.fold_in(key_list[10], 1), 0, BS - 1).astype(jnp.int32)
    inner_target = touch_ends(jax.random.randint(key_list[11], (NBLK, ELEM), 0, BS), jax.random.fold_in(key_list[11], 1), 0, BS - 1).astype(jnp.int32)
    inner_gain = jnp.clip(jnp.exp(math.log(0.5) - 2.3025851 * jax.random.uniform(key_list[12], (NBLK, ELEM), jnp.float32) ** steps_of(key_list[12], (NBLK, ELEM), ((0, 32),), -0.2, 0.2)), 0.05, 0.5)
    return dict(voltages=voltages, newton_steps=newton_steps, cap_diag=cap_diag, preconditioner=preconditioner, couple_block=couple_block, couple_owner=couple_owner, couple_offset=couple_offset, couple_source=couple_source, couple_target=couple_target, couple_gain=couple_gain, inner_source=inner_source, inner_target=inner_target, inner_gain=inner_gain)


def conductance(gain, first, second):
    drop = first - second
    rounded = lax.optimization_barrier((gain / (1.0 + drop * drop)).astype(jnp.bfloat16))
    return rounded.astype(jnp.float32)


def inner_image(source, target, weight, capacity, update):
    flat = jnp.zeros((BS * BS,), jnp.float32)
    flat = flat.at[source * BS + source].add(weight)
    flat = flat.at[target * BS + target].add(weight)
    flat = flat.at[source * BS + target].add(-weight)
    flat = flat.at[target * BS + source].add(-weight)
    matrix = flat.reshape(BS, BS) + jnp.diag(capacity)
    matrix = lax.optimization_barrier(matrix.astype(jnp.bfloat16)).astype(jnp.float32)
    return jnp.dot(matrix, update, precision=lax.Precision.HIGHEST)


def couple_image(source, target, weight, update):
    flat = jnp.zeros((BS * BS,), jnp.float32)
    flat = flat.at[target * BS + source].add(-weight)
    matrix = lax.optimization_barrier(flat.reshape(BS, BS).astype(jnp.bfloat16)).astype(jnp.float32)
    return jnp.dot(matrix, update, precision=lax.Precision.HIGHEST)


def grouped(func, group_count, arrays):
    shaped = tuple(item.reshape((group_count, item.shape[0] // group_count) + item.shape[1:]) for item in arrays)
    stacked = lax.map(lambda pieces: jax.vmap(func)(*pieces), shaped)
    return stacked.reshape((stacked.shape[0] * stacked.shape[1],) + stacked.shape[2:])


def reference(voltages, newton_steps, cap_diag, preconditioner, couple_block, couple_owner, couple_offset, couple_source, couple_target, couple_gain, inner_source, inner_target, inner_gain):
    group_count = N_DOM * N_SUB
    stamp_device = (jnp.arange(STAMPS, dtype=jnp.int32) // ST_DEV).astype(jnp.int32)
    column_block = (stamp_device * BLK_DEV + couple_block).astype(jnp.int32)
    row_block = (couple_owner[:, 0] * BLK_DEV + couple_offset).astype(jnp.int32)
    field = voltages
    results = []
    for newton in range(NEWTON):
        update = lax.optimization_barrier(newton_steps[newton].astype(jnp.bfloat16)).astype(jnp.float32)
        by_block = field.T
        update_rows = update.T
        inner_weight = conductance(inner_gain, jnp.take_along_axis(by_block, inner_source, axis=1), jnp.take_along_axis(by_block, inner_target, axis=1))
        inner_part = grouped(inner_image, group_count, (inner_source, inner_target, inner_weight, cap_diag.T, update_rows))
        local_rows = jnp.take_along_axis(by_block[column_block], couple_source, axis=1)
        remote_rows = jnp.take_along_axis(by_block[row_block], couple_target, axis=1)
        couple_weight = conductance(couple_gain, local_rows, remote_rows)
        images = grouped(couple_image, group_count, (couple_source, couple_target, couple_weight, update_rows[column_block]))
        couple_part = jax.ops.segment_sum(images, row_block, num_segments=NBLK)
        total = inner_part + couple_part
        results.append(jnp.einsum('ijr,rj->ir', preconditioner, total, precision=lax.Precision.HIGHEST))
        field = field + newton_steps[newton]
    return jnp.stack(results)
```

```python
import functools

import jax
import jax.numpy as jnp
from jax import lax
from jax.experimental import pallas as pl
from jax.experimental.pallas import tpu as pltpu
from jax.sharding import PartitionSpec as P

BS = 64
NEWTON = 2
LANES = 128
GROUP = 16
DIGIT = 8
AXES = ("dom", "sub")
NT = (((1,), (1,)), ((), ()))
TN = (((0,), (0,)), ((), ()))
NN = (((1,), (0,)), ((), ()))
F32 = jnp.float32
BF16 = jnp.bfloat16


def iota(shape, axis):
    return lax.broadcasted_iota(jnp.int32, shape, axis)


def dot(first, second, numbers):
    return lax.dot_general(first, second, numbers, preferred_element_type=F32)


def pick(table, index):
    return jnp.concatenate(
        [
            jnp.take_along_axis(table[r : r + 8], index[r : r + 8], axis=1)
            for r in range(0, table.shape[0], 8)
        ],
        axis=0,
    )


def conductance(gain, first, second):
    drop = first - second
    return gain / (1.0 + drop * drop)


def digits(index):
    high = lax.shift_right_logical(index, 3)
    return high.astype(F32).astype(BF16), (index - high * DIGIT).astype(F32).astype(BF16)


def hot_rows(digit, values):
    zero = jnp.zeros_like(values[0])
    masks = [digit == jnp.asarray(d, BF16) for d in range(DIGIT)]
    return jnp.concatenate([jnp.where(m, v, zero) for v in values for m in masks], axis=0)


def same_block(rows, columns):
    shape = (rows, columns)
    return (iota(shape, 0) % GROUP) == (iota(shape, 1) % GROUP)


def gather_nodes(spread):
    shape = (NEWTON * DIGIT * GROUP, LANES)
    column, lane = iota(shape, 0), iota(shape, 1)
    low = (column // GROUP) % DIGIT
    step = column // (GROUP * DIGIT)
    keep = low == lane % DIGIT
    if spread:
        keep = keep & (step == lane // BS)
    return keep.astype(F32).astype(BF16)


def fold_rows(wide):
    lane = iota((GROUP, LANES), 1) // DIGIT
    total = jnp.zeros((GROUP, LANES), F32)
    for s in range(NEWTON * DIGIT):
        total = total + jnp.where(lane == s, wide[s * GROUP : (s + 1) * GROUP], 0.0)
    return total


def split(value, parts):
    pieces = []
    for _ in range(parts):
        piece = value.astype(BF16)
        pieces.append(piece)
        value = value - piece.astype(F32)
    return pieces


def prepare_kernel(volt_ref, step_ref, cap_ref, send_ref, volt_out, update_out, cap_out):
    first = volt_ref[...]
    block_count = first.shape[1]
    step = step_ref[0]
    fields = jnp.concatenate([first, first + step], axis=0)
    updates = jnp.concatenate([step, step_ref[1]], axis=0).astype(BF16).astype(F32)
    caps = jnp.concatenate([cap_ref[...], cap_ref[...]], axis=0)
    field_rows = fields.T
    volt_out[...] = field_rows
    update_out[...] = updates.T
    cap_out[...] = caps.T
    packed = field_rows.astype(BF16)
    for d in range(send_ref.shape[0] // block_count):
        send_ref[pl.ds(d * block_count, block_count), :] = packed


def inner_kernel(volt_ref, update_ref, cap_ref, source_ref, target_ref, gain_ref, out_ref):
    block_count, elements = source_ref.shape
    nodes_any, nodes_step = gather_nodes(False), gather_nodes(True)
    images = []
    for start in range(0, block_count, GROUP):
        rows = slice(start, start + GROUP)
        volts, updates = volt_ref[rows, :], update_ref[rows, :]
        acc_ones = jnp.zeros((NEWTON * DIGIT * GROUP, DIGIT * GROUP), F32)
        acc = jnp.zeros((NEWTON * DIGIT * GROUP, NEWTON * DIGIT * GROUP), F32)
        for at in range(0, elements, LANES):
            lanes = slice(at, at + LANES)
            source, target = source_ref[rows, lanes], target_ref[rows, lanes]
            gain = jnp.where(source == target, 0.0, gain_ref[rows, lanes])
            weights, source_updates, target_updates = [], [], []
            for t in range(NEWTON):
                here, there = source + t * BS, target + t * BS
                weights.append(
                    conductance(gain, pick(volts, here), pick(volts, there)).astype(BF16)
                )
                source_updates.append(pick(updates, here).astype(BF16))
                target_updates.append(pick(updates, there).astype(BF16))
            ones = jnp.ones((GROUP, LANES), BF16)
            left, right, right_ones = [], [], []
            for index, others in ((source, target_updates), (target, source_updates)):
                high, low = digits(index)
                left.append(hot_rows(high, weights))
                right_ones.append(hot_rows(low, [ones]))
                right.append(hot_rows(low, others))
            left = jnp.concatenate(left, axis=1)
            acc_ones = acc_ones + dot(left, jnp.concatenate(right_ones, axis=1), NT)
            acc = acc + dot(left, jnp.concatenate(right, axis=1), NT)
        acc = jnp.where(same_block(*acc.shape), acc, 0.0)
        acc_ones = jnp.where(same_block(*acc_ones.shape), acc_ones, 0.0)
        diagonal = fold_rows(
            sum(dot(p, nodes_any[: DIGIT * GROUP], NN) for p in split(acc_ones, 2))
        )
        others = fold_rows(sum(dot(p, nodes_step, NN) for p in split(acc, 2)))
        diagonal = (diagonal + cap_ref[rows, :]).astype(BF16).astype(F32)
        images.append(diagonal * updates - others)
    out_ref[...] = jnp.concatenate(images, axis=0).T


def row_to_column(row):
    count = row.shape[1]
    shape = (count, count)
    return jnp.sum(jnp.where(iota(shape, 0) == iota(shape, 1), row, 0), axis=1, keepdims=True)


def column_to_row(column):
    count = column.shape[0]
    shape = (count, count)
    return jnp.sum(jnp.where(iota(shape, 0) == iota(shape, 1), column, 0), axis=0, keepdims=True)


def couple_kernel(
    per_owner,
    fields_ref,
    volt_ref,
    update_ref,
    block_ref,
    owner_ref,
    offset_ref,
    source_ref,
    target_ref,
    gain_ref,
    send_ref,
):
    stamp_count, elements = source_ref.shape
    block_count = volt_ref.shape[0]
    owner = owner_ref[...].astype(F32)
    offset = row_to_column(offset_ref[...].astype(F32))
    block = row_to_column(block_ref[...].astype(F32))
    owner_row = column_to_row(owner)

    row_hot = (
        iota((stamp_count, fields_ref.shape[0]), 1).astype(F32) == owner * block_count + offset
    )
    remote = dot(row_hot.astype(F32).astype(BF16), fields_ref[...], NN)
    block_hot = (iota((stamp_count, block_count), 1).astype(F32) == block).astype(F32).astype(BF16)
    high, middle, low = (dot(block_hot, p, NN) for p in split(volt_ref[...], 3))
    local = high + middle + low
    update = dot(block_hot, update_ref[...].astype(BF16), NN)

    nodes_step = gather_nodes(True)
    images = []
    for start in range(0, stamp_count, GROUP):
        rows = slice(start, start + GROUP)
        near, far, moved = local[rows], remote[rows], update[rows]
        acc = jnp.zeros((NEWTON * DIGIT * GROUP, NEWTON * DIGIT * GROUP), F32)
        left, right = [], []
        for at in range(0, elements, LANES):
            lanes = slice(at, at + LANES)
            source, target = source_ref[rows, lanes], target_ref[rows, lanes]
            gain = -gain_ref[rows, lanes]
            weights, updates = [], []
            for t in range(NEWTON):
                here, there = source + t * BS, target + t * BS
                weights.append(conductance(gain, pick(near, here), pick(far, there)).astype(BF16))
                updates.append(pick(moved, here).astype(BF16))
            high, low = digits(target)
            left.append(hot_rows(high, weights))
            right.append(hot_rows(low, updates))
            if len(left) == 2 or at + LANES >= elements:
                acc = acc + dot(
                    jnp.concatenate(left, axis=1), jnp.concatenate(right, axis=1), NT
                )
                left, right = [], []
        acc = jnp.where(same_block(*acc.shape), acc, 0.0).astype(BF16)
        images.append(fold_rows(dot(acc, nodes_step, NN)))
    images = jnp.concatenate(images, axis=0)

    shape = (stamp_count, stamp_count)
    earlier = (owner == owner_row) & (iota(shape, 0) < iota(shape, 1))
    rank_row = jnp.sum(jnp.where(earlier, 1.0, 0.0), axis=0, keepdims=True)
    slot_row = (owner_row * per_owner + rank_row) * NEWTON
    slots = jnp.concatenate([slot_row + t for t in range(NEWTON)], axis=1)
    place = iota((send_ref.shape[0], NEWTON * stamp_count), 0).astype(F32) == slots
    lane = iota((stamp_count, LANES), 1)
    offset_hot = jnp.where(lane.astype(F32) == offset, 1.0, 0.0)
    first = jnp.where(lane < BS, offset_hot, pltpu.roll(images, BS, 1))
    second = jnp.where(lane < BS, offset_hot, images)
    messages = jnp.concatenate([first, second], axis=0).astype(BF16)
    send_ref[...] = dot(place.astype(F32).astype(BF16), messages, NN).astype(BF16)


def finish_kernel(images_ref, inner_ref, precond_ref, out_ref):
    received = images_ref[...]
    block_count = inner_ref.shape[1]
    parity = iota(received.shape, 0) % NEWTON
    zero = jnp.zeros_like(received)
    for t in range(NEWTON):
        mine = jnp.where(parity == t, received.astype(F32), 0.0).astype(BF16)
        couple = dot(received, mine, TN)[BS:, :block_count]
        total = inner_ref[t * BS : (t + 1) * BS, :] + couple
        for i in range(0, BS, DIGIT):
            out_ref[t, i : i + DIGIT, :] = jnp.sum(
                precond_ref[i : i + DIGIT] * total[None], axis=1
            )


def call(kernel, out_shape, args, flops, bytes_accessed):
    spec = pl.BlockSpec(memory_space=pltpu.VMEM)
    several = isinstance(out_shape, (list, tuple))
    return pl.pallas_call(
        kernel,
        out_shape=out_shape,
        in_specs=[spec] * len(args),
        out_specs=[spec] * len(out_shape) if several else spec,
        compiler_params=pltpu.CompilerParams(vmem_limit_bytes=24 * 2**20),
        cost_estimate=pl.CostEstimate(
            flops=flops, bytes_accessed=bytes_accessed, transcendentals=0
        ),
    )(*args)


def exchange(rows, devices):
    shaped = rows.reshape((devices, rows.shape[0] // devices, rows.shape[1]))
    out = lax.all_to_all(shaped, AXES, split_axis=0, concat_axis=0, tiled=True)
    return out.reshape(rows.shape)


def per_device(
    voltages,
    newton_steps,
    cap_diag,
    preconditioner,
    couple_block,
    couple_owner,
    couple_offset,
    couple_source,
    couple_target,
    couple_gain,
    inner_source,
    inner_target,
    inner_gain,
):
    devices = lax.axis_size(AXES)
    stamp_count = couple_block.shape[0]
    block_count = voltages.shape[1]
    per_owner = max(2, 2 * stamp_count // devices)
    table = jax.ShapeDtypeStruct((block_count, LANES), F32)
    send, volts, updates, caps = call(
        prepare_kernel,
        [jax.ShapeDtypeStruct((devices * block_count, LANES), BF16), table, table, table],
        (voltages, newton_steps, cap_diag),
        10**5,
        10**5,
    )
    fields = exchange(send, devices)
    inner = call(
        inner_kernel,
        jax.ShapeDtypeStruct((NEWTON * BS, block_count), F32),
        (volts, updates, caps, inner_source, inner_target, inner_gain),
        4 * 10**9,
        10**6,
    )
    images = call(
        functools.partial(couple_kernel, per_owner),
        jax.ShapeDtypeStruct((devices * per_owner * NEWTON, LANES), BF16),
        (
            fields,
            volts,
            updates,
            couple_block.reshape(1, stamp_count),
            couple_owner,
            couple_offset.reshape(1, stamp_count),
            couple_source,
            couple_target,
            couple_gain,
        ),
        4 * 10**9,
        10**6,
    )
    received = exchange(images, devices)
    return call(
        finish_kernel,
        jax.ShapeDtypeStruct((NEWTON, BS, block_count), F32),
        (received, inner, preconditioner),
        10**8,
        2 * 10**6,
    )


def solution(mesh):
    in_specs = (
        P(None, AXES),
        P(None, None, AXES),
        P(None, AXES),
        P(None, None, AXES),
        P(AXES),
        P(AXES, None),
        P(AXES),
        P(AXES, None),
        P(AXES, None),
        P(AXES, None),
        P(AXES, None),
        P(AXES, None),
        P(AXES, None),
    )
    out_specs = P(None, None, AXES)
    return jax.shard_map(
        per_device, mesh=mesh, in_specs=in_specs, out_specs=out_specs, check_vma=False
    )
```

```python
import functools

import jax
import jax.numpy as jnp
from jax import lax
from jax.experimental import pallas as pl
from jax.experimental.pallas import tpu as pltpu
from jax.sharding import PartitionSpec as P

BS = 64
NEWTON = 2
LANES = 128
GROUP = 16
DIGIT = 8
AXES = ("dom", "sub")
NT = (((1,), (1,)), ((), ()))
TN = (((0,), (0,)), ((), ()))
NN = (((1,), (0,)), ((), ()))
F32 = jnp.float32
BF16 = jnp.bfloat16


def iota(shape, axis):
    return lax.broadcasted_iota(jnp.int32, shape, axis)


def dot(first, second, numbers):
    return lax.dot_general(first, second, numbers, preferred_element_type=F32)


def pick(table, index):
    return jnp.concatenate(
        [
            jnp.take_along_axis(table[r : r + 8], index[r : r + 8], axis=1)
            for r in range(0, table.shape[0], 8)
        ],
        axis=0,
    )


def conductance(gain, first, second):
    drop = first - second
    return gain / (1.0 + drop * drop)


def digits(index):
    high = lax.shift_right_logical(index, 3)
    return high.astype(F32).astype(BF16), (index - high * DIGIT).astype(F32).astype(BF16)


def hot_rows(digit, values):
    zero = jnp.zeros_like(values[0])
    masks = [digit == jnp.asarray(d, BF16) for d in range(DIGIT)]
    return jnp.concatenate([jnp.where(m, v, zero) for v in values for m in masks], axis=0)


def same_block(rows, columns):
    shape = (rows, columns)
    return (iota(shape, 0) % GROUP) == (iota(shape, 1) % GROUP)


def gather_nodes(spread):
    shape = (NEWTON * DIGIT * GROUP, LANES)
    column, lane = iota(shape, 0), iota(shape, 1)
    low = (column // GROUP) % DIGIT
    step = column // (GROUP * DIGIT)
    keep = low == lane % DIGIT
    if spread:
        keep = keep & (step == lane // BS)
    return keep.astype(F32).astype(BF16)


def fold_rows(wide):
    lane = iota((GROUP, LANES), 1) // DIGIT
    total = jnp.zeros((GROUP, LANES), F32)
    for s in range(NEWTON * DIGIT):
        total = total + jnp.where(lane == s, wide[s * GROUP : (s + 1) * GROUP], 0.0)
    return total


def split(value, parts):
    pieces = []
    for _ in range(parts):
        piece = value.astype(BF16)
        pieces.append(piece)
        value = value - piece.astype(F32)
    return pieces


def fields_of(table_ref):
    first = table_ref[0]
    return jnp.concatenate([first, first + table_ref[1]], axis=1)


def prepare_kernel(table_ref, send_ref):
    packed = fields_of(table_ref).astype(BF16)
    block_count = packed.shape[0]
    for d in range(send_ref.shape[0] // block_count):
        send_ref[pl.ds(d * block_count, block_count), :] = packed


def inner_images(volt_rows, update_rows, cap_rows, source_ref, target_ref, gain_ref):
    block_count, elements = source_ref.shape
    nodes_any, nodes_step = gather_nodes(False), gather_nodes(True)
    images = []
    for start in range(0, block_count, GROUP):
        rows = slice(start, start + GROUP)
        volts, updates = volt_rows[rows], update_rows[rows]
        acc_ones = jnp.zeros((NEWTON * DIGIT * GROUP, DIGIT * GROUP), F32)
        acc = jnp.zeros((NEWTON * DIGIT * GROUP, NEWTON * DIGIT * GROUP), F32)
        for at in range(0, elements, LANES):
            lanes = slice(at, at + LANES)
            source, target = source_ref[rows, lanes], target_ref[rows, lanes]
            gain = jnp.where(source == target, 0.0, gain_ref[rows, lanes])
            weights, source_updates, target_updates = [], [], []
            for t in range(NEWTON):
                here, there = source + t * BS, target + t * BS
                weights.append(
                    conductance(gain, pick(volts, here), pick(volts, there)).astype(BF16)
                )
                source_updates.append(pick(updates, here).astype(BF16))
                target_updates.append(pick(updates, there).astype(BF16))
            ones = jnp.ones((GROUP, LANES), BF16)
            left, right, right_ones = [], [], []
            for index, others in ((source, target_updates), (target, source_updates)):
                high, low = digits(index)
                left.append(hot_rows(high, weights))
                right_ones.append(hot_rows(low, [ones]))
                right.append(hot_rows(low, others))
            left = jnp.concatenate(left, axis=1)
            acc_ones = acc_ones + dot(left, jnp.concatenate(right_ones, axis=1), NT)
            acc = acc + dot(left, jnp.concatenate(right, axis=1), NT)
        acc = jnp.where(same_block(*acc.shape), acc, 0.0)
        acc_ones = jnp.where(same_block(*acc_ones.shape), acc_ones, 0.0)
        diagonal = fold_rows(
            sum(dot(p, nodes_any[: DIGIT * GROUP], NN) for p in split(acc_ones, 2))
        )
        others = fold_rows(sum(dot(p, nodes_step, NN) for p in split(acc, 2)))
        diagonal = (diagonal + cap_rows[rows]).astype(BF16).astype(F32)
        images.append(diagonal * updates - others)
    return jnp.concatenate(images, axis=0)


def row_to_column(row):
    count = row.shape[1]
    shape = (count, count)
    return jnp.sum(jnp.where(iota(shape, 0) == iota(shape, 1), row, 0), axis=1, keepdims=True)


def local_kernel(
    per_owner,
    table_ref,
    cap_ref,
    block_ref,
    owner_ref,
    offset_ref,
    inner_source_ref,
    inner_target_ref,
    inner_gain_ref,
    source_ref,
    target_ref,
    gain_ref,
    inner_ref,
    target_out,
    gain_out,
    near_ref,
    moved_ref,
    row_hot_ref,
    place_ref,
    offset_hot_ref,
):
    stamp_count, elements = source_ref.shape
    block_count = table_ref.shape[1]
    target_out[...] = target_ref[...]
    gain_out[...] = gain_ref[...]
    volt_rows = fields_of(table_ref)
    updates = jnp.concatenate([table_ref[1], table_ref[2]], axis=1).astype(BF16)
    caps = jnp.concatenate([cap_ref[...], cap_ref[...]], axis=1)

    owner_row = owner_ref[...].astype(F32)
    owner = row_to_column(owner_row)
    offset = row_to_column(offset_ref[...].astype(F32))
    block = row_to_column(block_ref[...].astype(F32))
    row_hot = iota(row_hot_ref.shape, 1).astype(F32) == owner * block_count + offset
    row_hot_ref[...] = row_hot.astype(F32).astype(BF16)
    shape = (stamp_count, stamp_count)
    earlier = (owner == owner_row) & (iota(shape, 0) < iota(shape, 1))
    rank_row = jnp.sum(jnp.where(earlier, 1.0, 0.0), axis=0, keepdims=True)
    slot_row = (owner_row * per_owner + rank_row) * NEWTON
    slots = jnp.concatenate([slot_row + t for t in range(NEWTON)], axis=1)
    place_ref[...] = (iota(place_ref.shape, 0).astype(F32) == slots).astype(F32).astype(BF16)
    offset_hot_ref[...] = jnp.where(
        iota(offset_hot_ref.shape, 1).astype(F32) == offset, 1.0, 0.0
    )

    block_hot = (iota((stamp_count, block_count), 1).astype(F32) == block).astype(F32).astype(BF16)
    local = sum(dot(block_hot, p, NN) for p in split(volt_rows, 3))
    moved = dot(block_hot, updates, NN)
    for start in range(0, stamp_count, GROUP):
        rows = slice(start, start + GROUP)
        for at in range(0, elements, LANES):
            lanes = slice(at, at + LANES)
            source = source_ref[rows, lanes]
            for t in range(NEWTON):
                here = source + t * BS
                near_ref[t, rows, lanes] = pick(local[rows], here)
                moved_ref[t, rows, lanes] = pick(moved[rows], here).astype(BF16)
    inner_ref[...] = inner_images(
        volt_rows, updates.astype(F32), caps, inner_source_ref, inner_target_ref, inner_gain_ref
    ).T


def couple_kernel(
    fields_ref,
    target_ref,
    gain_ref,
    near_ref,
    moved_ref,
    row_hot_ref,
    place_ref,
    offset_hot_ref,
    send_ref,
):
    stamp_count, elements = target_ref.shape
    remote = dot(row_hot_ref[...], fields_ref[...], NN)
    nodes_step = gather_nodes(True)
    images = []
    for start in range(0, stamp_count, GROUP):
        rows = slice(start, start + GROUP)
        far = remote[rows]
        acc = jnp.zeros((NEWTON * DIGIT * GROUP, NEWTON * DIGIT * GROUP), F32)
        left, right = [], []
        for at in range(0, elements, LANES):
            lanes = slice(at, at + LANES)
            target = target_ref[rows, lanes]
            gain = -gain_ref[rows, lanes]
            weights = [
                conductance(gain, near_ref[t, rows, lanes], pick(far, target + t * BS)).astype(BF16)
                for t in range(NEWTON)
            ]
            high, low = digits(target)
            left.append(hot_rows(high, weights))
            right.append(hot_rows(low, [moved_ref[t, rows, lanes] for t in range(NEWTON)]))
            if len(left) == 2 or at + LANES >= elements:
                acc = acc + dot(
                    jnp.concatenate(left, axis=1), jnp.concatenate(right, axis=1), NT
                )
                left, right = [], []
        acc = jnp.where(same_block(*acc.shape), acc, 0.0).astype(BF16)
        images.append(fold_rows(dot(acc, nodes_step, NN)))
    images = jnp.concatenate(images, axis=0)
    lane = iota(images.shape, 1)
    messages = jnp.concatenate(
        [
            jnp.where(lane < BS, offset_hot_ref[...], pltpu.roll(images, BS, 1)),
            jnp.where(lane < BS, offset_hot_ref[...], images),
        ],
        axis=0,
    ).astype(BF16)
    send_ref[...] = dot(place_ref[...], messages, NN).astype(BF16)


def finish_kernel(images_ref, inner_ref, precond_ref, out_ref):
    received = images_ref[...]
    block_count = inner_ref.shape[1]
    parity = iota(received.shape, 0) % NEWTON
    for t in range(NEWTON):
        mine = jnp.where(parity == t, received.astype(F32), 0.0).astype(BF16)
        couple = dot(received, mine, TN)[BS:, :block_count]
        total = inner_ref[t * BS : (t + 1) * BS, :] + couple
        rows = [
            jnp.sum(precond_ref[i : i + DIGIT] * total[None], axis=1)
            for i in range(0, BS, DIGIT)
        ]
        out_ref[t] = jnp.concatenate(rows, axis=0).T


def call(kernel, out_shape, args, flops):
    spec = pl.BlockSpec(memory_space=pltpu.VMEM)
    several = isinstance(out_shape, (list, tuple))
    return pl.pallas_call(
        kernel,
        out_shape=out_shape,
        in_specs=[spec] * len(args),
        out_specs=[spec] * len(out_shape) if several else spec,
        compiler_params=pltpu.CompilerParams(vmem_limit_bytes=24 * 2**20),
        cost_estimate=pl.CostEstimate(flops=flops, bytes_accessed=10**6, transcendentals=0),
    )(*args)


def exchange(rows, devices):
    shaped = rows.reshape((devices, rows.shape[0] // devices, rows.shape[1]))
    out = lax.all_to_all(shaped, AXES, split_axis=0, concat_axis=0, tiled=True)
    return out.reshape(rows.shape)


def per_device(
    voltages,
    newton_steps,
    cap_diag,
    preconditioner,
    couple_block,
    couple_owner,
    couple_offset,
    couple_source,
    couple_target,
    couple_gain,
    inner_source,
    inner_target,
    inner_gain,
):
    devices = lax.axis_size(AXES)
    stamp_count, elements = couple_source.shape
    block_count = voltages.shape[1]
    per_owner = max(2, 2 * stamp_count // devices)
    row_count = devices * per_owner * NEWTON
    like = jax.ShapeDtypeStruct
    table = jnp.concatenate([voltages.T[None], newton_steps.transpose(0, 2, 1)], axis=0)
    send = call(
        prepare_kernel, like((devices * block_count, LANES), BF16), (table,), 2 * 10**10
    )
    fields = exchange(send, devices)
    inner, *prepared = call(
        functools.partial(local_kernel, per_owner),
        [
            like((NEWTON * BS, block_count), F32),
            like(couple_target.shape, couple_target.dtype),
            like(couple_gain.shape, couple_gain.dtype),
            like((NEWTON, stamp_count, elements), F32),
            like((NEWTON, stamp_count, elements), BF16),
            like((stamp_count, devices * block_count), BF16),
            like((row_count, NEWTON * stamp_count), BF16),
            like((stamp_count, LANES), F32),
        ],
        (
            table,
            cap_diag.T,
            couple_block.reshape(1, stamp_count),
            couple_owner.reshape(1, stamp_count),
            couple_offset.reshape(1, stamp_count),
            inner_source,
            inner_target,
            inner_gain,
            couple_source,
            couple_target,
            couple_gain,
        ),
        2 * 10**10,
    )
    images = call(
        couple_kernel, like((row_count, LANES), BF16), (fields, *prepared), 4 * 10**9
    )
    received = exchange(images, devices)
    out = call(
        finish_kernel,
        like((NEWTON, block_count, BS), F32),
        (received, inner, preconditioner),
        10**8,
    )
    return out.transpose(0, 2, 1)


def solution(mesh):
    in_specs = (
        P(None, AXES),
        P(None, None, AXES),
        P(None, AXES),
        P(None, None, AXES),
        P(AXES),
        P(AXES, None),
        P(AXES),
        P(AXES, None),
        P(AXES, None),
        P(AXES, None),
        P(AXES, None),
        P(AXES, None),
        P(AXES, None),
    )
    out_specs = P(None, None, AXES)
    return jax.shard_map(
        per_device, mesh=mesh, in_specs=in_specs, out_specs=out_specs, check_vma=False
    )
```

```python
import functools

import jax
import jax.numpy as jnp
from jax import lax
from jax.experimental import pallas as pl
from jax.experimental.pallas import tpu as pltpu
from jax.sharding import PartitionSpec as P

BS = 64
NEWTON = 2
LANES = 128
GROUP = 16
DIGIT = 8
AXES = ("dom", "sub")
NT = (((1,), (1,)), ((), ()))
TN = (((0,), (0,)), ((), ()))
NN = (((1,), (0,)), ((), ()))
F32 = jnp.float32
BF16 = jnp.bfloat16


def iota(shape, axis):
    return lax.broadcasted_iota(jnp.int32, shape, axis)


def dot(first, second, numbers):
    return lax.dot_general(first, second, numbers, preferred_element_type=F32)


def pick(table, index):
    return jnp.concatenate(
        [
            jnp.take_along_axis(table[r : r + 8], index[r : r + 8], axis=1)
            for r in range(0, table.shape[0], 8)
        ],
        axis=0,
    )


def conductance(gain, first, second):
    drop = first - second
    return gain / (1.0 + drop * drop)


def digits(index):
    high = lax.shift_right_logical(index, 3)
    return high.astype(F32).astype(BF16), (index - high * DIGIT).astype(F32).astype(BF16)


def hot_rows(digit, values):
    zero = jnp.zeros_like(values[0])
    masks = [digit == jnp.asarray(d, BF16) for d in range(DIGIT)]
    return jnp.concatenate([jnp.where(m, v, zero) for v in values for m in masks], axis=0)


def same_block(shape, group):
    return (iota(shape, 0) % group) == (iota(shape, 1) % group)


def gather_nodes(spread):
    shape = (NEWTON * DIGIT * GROUP, LANES)
    column, lane = iota(shape, 0), iota(shape, 1)
    low = (column // GROUP) % DIGIT
    step = column // (GROUP * DIGIT)
    keep = low == lane % DIGIT
    if spread:
        keep = keep & (step == lane // BS)
    return keep.astype(F32).astype(BF16)


def fold_rows(wide):
    lane = iota((GROUP, LANES), 1) // DIGIT
    total = jnp.zeros((GROUP, LANES), F32)
    for s in range(NEWTON * DIGIT):
        total = total + jnp.where(lane == s, wide[s * GROUP : (s + 1) * GROUP], 0.0)
    return total


def split(value, parts):
    pieces = []
    for _ in range(parts):
        piece = value.astype(BF16)
        pieces.append(piece)
        value = value - piece.astype(F32)
    return pieces


def fields_of(table_ref):
    first = table_ref[0]
    return jnp.concatenate([first, first + table_ref[1]], axis=1)


def prepare_kernel(table_ref, send_ref):
    block_count = table_ref.shape[1]
    half = block_count // 2
    first = table_ref[0]
    packed = [
        jnp.concatenate([field[:half], field[half:]], axis=1).astype(BF16)
        for field in (first, first + table_ref[1])
    ]
    for d in range(send_ref.shape[0] // half):
        send_ref[pl.ds(d * half, half), :] = packed[d % NEWTON]


def inner_images(volt_rows, update_rows, cap_rows, source_ref, target_ref, gain_ref):
    block_count, elements = source_ref.shape
    nodes_any, nodes_step = gather_nodes(False), gather_nodes(True)
    images = []
    for start in range(0, block_count, GROUP):
        rows = slice(start, start + GROUP)
        volts, updates = volt_rows[rows], update_rows[rows]
        acc_ones = jnp.zeros((NEWTON * DIGIT * GROUP, DIGIT * GROUP), F32)
        acc = jnp.zeros((NEWTON * DIGIT * GROUP, NEWTON * DIGIT * GROUP), F32)
        for at in range(0, elements, LANES):
            lanes = slice(at, at + LANES)
            source, target = source_ref[rows, lanes], target_ref[rows, lanes]
            gain = jnp.where(source == target, 0.0, gain_ref[rows, lanes])
            weights, source_updates, target_updates = [], [], []
            for t in range(NEWTON):
                here, there = source + t * BS, target + t * BS
                weights.append(
                    conductance(gain, pick(volts, here), pick(volts, there)).astype(BF16)
                )
                source_updates.append(pick(updates, here).astype(BF16))
                target_updates.append(pick(updates, there).astype(BF16))
            ones = jnp.ones((GROUP, LANES), BF16)
            left, right, right_ones = [], [], []
            for index, others in ((source, target_updates), (target, source_updates)):
                high, low = digits(index)
                left.append(hot_rows(high, weights))
                right_ones.append(hot_rows(low, [ones]))
                right.append(hot_rows(low, others))
            left = jnp.concatenate(left, axis=1)
            acc_ones = acc_ones + dot(left, jnp.concatenate(right_ones, axis=1), NT)
            acc = acc + dot(left, jnp.concatenate(right, axis=1), NT)
        acc = jnp.where(same_block(acc.shape, GROUP), acc, 0.0)
        acc_ones = jnp.where(same_block(acc_ones.shape, GROUP), acc_ones, 0.0)
        diagonal = fold_rows(
            sum(dot(p, nodes_any[: DIGIT * GROUP], NN) for p in split(acc_ones, 2))
        )
        others = fold_rows(sum(dot(p, nodes_step, NN) for p in split(acc, 2)))
        diagonal = (diagonal + cap_rows[rows]).astype(BF16).astype(F32)
        images.append(diagonal * updates - others)
    return jnp.concatenate(images, axis=0)


def row_to_column(row):
    count = row.shape[1]
    shape = (count, count)
    return jnp.sum(jnp.where(iota(shape, 0) == iota(shape, 1), row, 0), axis=1, keepdims=True)


def inner_kernel(
    table_ref, cap_ref, inner_source_ref, inner_target_ref, inner_gain_ref, inner_ref
):
    updates = jnp.concatenate([table_ref[1], table_ref[2]], axis=1).astype(BF16).astype(F32)
    caps = jnp.concatenate([cap_ref[...], cap_ref[...]], axis=1)
    inner_ref[...] = inner_images(
        fields_of(table_ref), updates, caps, inner_source_ref, inner_target_ref, inner_gain_ref
    ).T


def stamp_kernel(
    per_owner,
    facts_ref,
    facts_other,
    table_ref,
    table_other,
    source_ref,
    source_other,
    target_ref,
    target_other,
    gain_ref,
    gain_other,
    target_out,
    gain_out,
    near_ref,
    moved_ref,
    row_hot_ref,
    place_ref,
    offset_hot_ref,
):
    own_count, elements = source_ref.shape
    stamp_count = 2 * own_count
    block_count = table_ref.shape[1]
    half = block_count // 2
    later = lax.axis_index("sub") == 1
    tables = []
    for ref in (table_ref, table_other):
        field = jnp.where(later, ref[0] + ref[1], ref[0])
        update = jnp.where(later, ref[2], ref[1]).astype(BF16).astype(F32)
        tables.append(jnp.concatenate([field, update], axis=1))
    tables = jnp.concatenate(tables, axis=0)

    facts = jnp.concatenate([facts_ref[...], facts_other[...]], axis=1).astype(F32)
    block_row, owner_row, offset_row = facts[0:1], facts[1:2], facts[2:3]
    mine = iota((1, stamp_count), 1) < own_count
    block = row_to_column(jnp.where(mine, block_row, block_row + block_count))
    owner = row_to_column(owner_row)
    offset = row_to_column(offset_row)
    place_in_half = jnp.where(offset < half, offset, offset - half)
    row_hot = iota(row_hot_ref.shape, 1).astype(F32) == owner * half + place_in_half
    row_hot_ref[...] = row_hot.astype(F32).astype(BF16)
    shape = (stamp_count, stamp_count)
    row, column = iota(shape, 0), iota(shape, 1)
    earlier = (owner == owner_row) & (row < column) & ((row < own_count) == (column < own_count))
    rank_row = jnp.sum(jnp.where(earlier, 1.0, 0.0), axis=0, keepdims=True)
    rank_row = jnp.where(mine, rank_row, rank_row + per_owner)
    slot_row = owner_row * (2 * per_owner) + rank_row
    place = iota(place_ref.shape, 0).astype(F32) == slot_row
    place_ref[...] = place.astype(F32).astype(BF16)
    offset_hot_ref[...] = jnp.where(
        iota(offset_hot_ref.shape, 1).astype(F32) == offset, 1.0, 0.0
    )

    block_hot = iota((stamp_count, 2 * block_count), 1).astype(F32) == block
    block_hot = block_hot.astype(F32).astype(BF16)
    local = sum(dot(block_hot, p, NN) for p in split(tables, 3))
    for n, (sources, targets, gains) in enumerate(
        ((source_ref, target_ref, gain_ref), (source_other, target_other, gain_other))
    ):
        held = slice(n * own_count, (n + 1) * own_count)
        target_out[held, :] = targets[...]
        gain_out[held, :] = gains[...]
        near = local[held]
        for at in range(0, elements, LANES):
            lanes = slice(at, at + LANES)
            source = sources[:, lanes]
            near_ref[held, lanes] = pick(near, source)
            moved_ref[held, lanes] = pick(near, source + BS).astype(BF16)


def couple_kernel(
    half,
    fields_ref,
    target_ref,
    gain_ref,
    near_ref,
    moved_ref,
    row_hot_ref,
    place_ref,
    offset_hot_ref,
    send_ref,
):
    stamp_count, elements = target_ref.shape
    group = NEWTON * GROUP
    offset_hot = offset_hot_ref[...]
    lane = iota(offset_hot.shape, 1)
    remote = dot(row_hot_ref[...], fields_ref[...], NN)
    upper = jnp.sum(
        jnp.where(lane >= half, offset_hot, 0.0), axis=1, keepdims=True
    )
    remote = jnp.where(upper > 0.5, pltpu.roll(remote, BS, 1), remote)
    shape = (DIGIT * group, LANES)
    node = iota(shape, 1) - BS
    nodes = (node >= 0) & (node % DIGIT == iota(shape, 0) // group)
    nodes = nodes.astype(F32).astype(BF16)
    high_lane = (iota((group, LANES), 1) - BS) // DIGIT
    images = []
    for start in range(0, stamp_count, group):
        rows = slice(start, start + group)
        far = remote[rows]
        acc = jnp.zeros((DIGIT * group, DIGIT * group), F32)
        left, right = [], []
        for at in range(0, elements, LANES):
            lanes = slice(at, at + LANES)
            target = target_ref[rows, lanes]
            weight = conductance(-gain_ref[rows, lanes], near_ref[rows, lanes], pick(far, target))
            high, low = digits(target)
            left.append(hot_rows(high, [weight.astype(BF16)]))
            right.append(hot_rows(low, [moved_ref[rows, lanes]]))
            if len(left) == 2 or at + LANES >= elements:
                acc = acc + dot(
                    jnp.concatenate(left, axis=1), jnp.concatenate(right, axis=1), NT
                )
                left, right = [], []
        acc = jnp.where(same_block(acc.shape, group), acc, 0.0).astype(BF16)
        wide = dot(acc, nodes, NN)
        total = jnp.zeros((group, LANES), F32)
        for h in range(DIGIT):
            total = total + jnp.where(high_lane == h, wide[h * group : (h + 1) * group], 0.0)
        images.append(total)
    images = jnp.concatenate(images, axis=0)
    messages = jnp.where(lane < BS, offset_hot, images).astype(BF16)
    send_ref[...] = dot(place_ref[...], messages, NN).astype(BF16)


def finish_kernel(row_count, images_ref, inner_ref, precond_ref, out_ref):
    received = images_ref[...]
    block_count = inner_ref.shape[1]
    step = iota(received.shape, 0) // row_count % NEWTON
    for t in range(NEWTON):
        mine = jnp.where(step == t, received.astype(F32), 0.0).astype(BF16)
        couple = dot(received, mine, TN)[BS:, :block_count]
        total = inner_ref[t * BS : (t + 1) * BS, :] + couple
        rows = [
            jnp.sum(precond_ref[i : i + DIGIT] * total[None], axis=1)
            for i in range(0, BS, DIGIT)
        ]
        out_ref[t] = jnp.concatenate(rows, axis=0).T


def call(kernel, out_shape, args, flops):
    spec = pl.BlockSpec(memory_space=pltpu.VMEM)
    several = isinstance(out_shape, (list, tuple))
    return pl.pallas_call(
        kernel,
        out_shape=out_shape,
        in_specs=[spec] * len(args),
        out_specs=[spec] * len(out_shape) if several else spec,
        compiler_params=pltpu.CompilerParams(vmem_limit_bytes=24 * 2**20),
        cost_estimate=pl.CostEstimate(flops=flops, bytes_accessed=10**6, transcendentals=0),
    )(*args)


def exchange(rows, devices):
    shaped = rows.reshape((devices, rows.shape[0] // devices, rows.shape[1]))
    out = lax.all_to_all(shaped, AXES, split_axis=0, concat_axis=0, tiled=True)
    return out.reshape(rows.shape)


def per_device(
    voltages,
    newton_steps,
    cap_diag,
    preconditioner,
    couple_block,
    couple_owner,
    couple_offset,
    couple_source,
    couple_target,
    couple_gain,
    inner_source,
    inner_target,
    inner_gain,
):
    devices = lax.axis_size(AXES)
    stamp_count, elements = couple_source.shape
    block_count = voltages.shape[1]
    per_owner = max(2, 2 * stamp_count // devices)
    row_count = devices * per_owner * NEWTON
    like = jax.ShapeDtypeStruct
    swap = lambda array: lax.ppermute(array, "sub", [(0, 1), (1, 0)])
    table = jnp.concatenate([voltages.T[None], newton_steps.transpose(0, 2, 1)], axis=0)
    send = call(
        prepare_kernel, like((devices * block_count // 2, LANES), BF16), (table,), 2 * 10**10
    )
    fields = exchange(send, devices)
    inner = call(
        inner_kernel,
        like((NEWTON * BS, block_count), F32),
        (table, cap_diag.T, inner_source, inner_target, inner_gain),
        4 * 10**9,
    )
    facts = [fact.reshape(1, stamp_count) for fact in (couple_block, couple_owner, couple_offset)]
    wanted = (jnp.concatenate(facts, axis=0), table, couple_source, couple_target, couple_gain)
    pairs = [half for array in wanted for half in (array, swap(array))]
    both = 2 * stamp_count
    prepared = call(
        functools.partial(stamp_kernel, per_owner),
        [
            like((both, elements), couple_target.dtype),
            like((both, elements), couple_gain.dtype),
            like((both, elements), F32),
            like((both, elements), BF16),
            like((both, devices * block_count // 2), BF16),
            like((row_count, both), BF16),
            like((both, LANES), F32),
        ],
        pairs,
        10**8,
    )
    images = call(
        functools.partial(couple_kernel, block_count // 2),
        like((row_count, LANES), BF16),
        (fields, *prepared),
        4 * 10**9,
    )
    received = exchange(images, devices)
    out = call(
        functools.partial(finish_kernel, 2 * per_owner),
        like((NEWTON, block_count, BS), F32),
        (received, inner, preconditioner),
        10**8,
    )
    return out.transpose(0, 2, 1)


def solution(mesh):
    in_specs = (
        P(None, AXES),
        P(None, None, AXES),
        P(None, AXES),
        P(None, None, AXES),
        P(AXES),
        P(AXES, None),
        P(AXES),
        P(AXES, None),
        P(AXES, None),
        P(AXES, None),
        P(AXES, None),
        P(AXES, None),
        P(AXES, None),
    )
    out_specs = P(None, None, AXES)
    return jax.shard_map(
        per_device, mesh=mesh, in_specs=in_specs, out_specs=out_specs, check_vma=False
    )
```

```python
import functools

import jax
import jax.numpy as jnp
from jax import lax
from jax.experimental import pallas as pl
from jax.experimental.pallas import tpu as pltpu
from jax.sharding import PartitionSpec as P

BS = 64
NEWTON = 2
LANES = 128
GROUP = 16
DIGIT = 8
AXES = ("dom", "sub")
NT = (((1,), (1,)), ((), ()))
TN = (((0,), (0,)), ((), ()))
NN = (((1,), (0,)), ((), ()))
F32 = jnp.float32
BF16 = jnp.bfloat16


def iota(shape, axis):
    return lax.broadcasted_iota(jnp.int32, shape, axis)


def dot(first, second, numbers):
    return lax.dot_general(first, second, numbers, preferred_element_type=F32)


def pick(table, index):
    return jnp.concatenate(
        [
            jnp.take_along_axis(table[r : r + 8], index[r : r + 8], axis=1)
            for r in range(0, table.shape[0], 8)
        ],
        axis=0,
    )


def conductance(gain, first, second):
    drop = first - second
    return gain / (1.0 + drop * drop)


def digits(index):
    high = lax.shift_right_logical(index, 3)
    return high.astype(F32).astype(BF16), (index - high * DIGIT).astype(F32).astype(BF16)


def hot_rows(digit, values):
    zero = jnp.zeros_like(values[0])
    masks = [digit == jnp.asarray(d, BF16) for d in range(DIGIT)]
    return jnp.concatenate([jnp.where(m, v, zero) for v in values for m in masks], axis=0)


def same_block(shape, group):
    return (iota(shape, 0) % group) == (iota(shape, 1) % group)


def gather_nodes(spread):
    shape = (NEWTON * DIGIT * GROUP, LANES)
    column, lane = iota(shape, 0), iota(shape, 1)
    low = (column // GROUP) % DIGIT
    step = column // (GROUP * DIGIT)
    keep = low == lane % DIGIT
    if spread:
        keep = keep & (step == lane // BS)
    return keep.astype(F32).astype(BF16)


def fold_rows(wide):
    lane = iota((GROUP, LANES), 1) // DIGIT
    total = jnp.zeros((GROUP, LANES), F32)
    for s in range(NEWTON * DIGIT):
        total = total + jnp.where(lane == s, wide[s * GROUP : (s + 1) * GROUP], 0.0)
    return total


def split(value, parts):
    pieces = []
    for _ in range(parts):
        piece = value.astype(BF16)
        pieces.append(piece)
        value = value - piece.astype(F32)
    return pieces


def fields_of(table_ref):
    first = table_ref[0]
    return jnp.concatenate([first, first + table_ref[1]], axis=1)


def prepare_kernel(table_ref, send_ref):
    block_count = table_ref.shape[1]
    half = block_count // 2
    first = table_ref[0]
    packed = [
        jnp.concatenate([field[:half], field[half:]], axis=1).astype(BF16)
        for field in (first, first + table_ref[1])
    ]
    for d in range(send_ref.shape[0] // half):
        send_ref[pl.ds(d * half, half), :] = packed[d % NEWTON]


def inner_images(volt_rows, update_rows, cap_rows, source_ref, target_ref, gain_ref):
    block_count, elements = source_ref.shape
    nodes_any, nodes_step = gather_nodes(False), gather_nodes(True)
    images = []
    for start in range(0, block_count, GROUP):
        rows = slice(start, start + GROUP)
        volts, updates = volt_rows[rows], update_rows[rows]
        acc_ones = jnp.zeros((NEWTON * DIGIT * GROUP, DIGIT * GROUP), F32)
        acc = jnp.zeros((NEWTON * DIGIT * GROUP, NEWTON * DIGIT * GROUP), F32)
        for at in range(0, elements, LANES):
            lanes = slice(at, at + LANES)
            source, target = source_ref[rows, lanes], target_ref[rows, lanes]
            gain = jnp.where(source == target, 0.0, gain_ref[rows, lanes])
            weights, source_updates, target_updates = [], [], []
            for t in range(NEWTON):
                here, there = source + t * BS, target + t * BS
                weights.append(
                    conductance(gain, pick(volts, here), pick(volts, there)).astype(BF16)
                )
                source_updates.append(pick(updates, here).astype(BF16))
                target_updates.append(pick(updates, there).astype(BF16))
            ones = jnp.ones((GROUP, LANES), BF16)
            left, right, right_ones = [], [], []
            for index, others in ((source, target_updates), (target, source_updates)):
                high, low = digits(index)
                left.append(hot_rows(high, weights))
                right_ones.append(hot_rows(low, [ones]))
                right.append(hot_rows(low, others))
            left = jnp.concatenate(left, axis=1)
            acc_ones = acc_ones + dot(left, jnp.concatenate(right_ones, axis=1), NT)
            acc = acc + dot(left, jnp.concatenate(right, axis=1), NT)
        acc = jnp.where(same_block(acc.shape, GROUP), acc, 0.0)
        acc_ones = jnp.where(same_block(acc_ones.shape, GROUP), acc_ones, 0.0)
        diagonal = fold_rows(
            sum(dot(p, nodes_any[: DIGIT * GROUP], NN) for p in split(acc_ones, 2))
        )
        others = fold_rows(sum(dot(p, nodes_step, NN) for p in split(acc, 2)))
        diagonal = (diagonal + cap_rows[rows]).astype(BF16).astype(F32)
        images.append(diagonal * updates - others)
    return jnp.concatenate(images, axis=0)


def row_to_column(row):
    count = row.shape[1]
    shape = (count, count)
    return jnp.sum(jnp.where(iota(shape, 0) == iota(shape, 1), row, 0), axis=1, keepdims=True)


def inner_kernel(
    table_ref,
    cap_ref,
    inner_source_ref,
    inner_target_ref,
    inner_gain_ref,
    inner_ref,
):
    updates = jnp.concatenate([table_ref[1], table_ref[2]], axis=1).astype(BF16).astype(F32)
    caps = jnp.concatenate([cap_ref[...], cap_ref[...]], axis=1)
    inner_ref[...] = inner_images(
        fields_of(table_ref), updates, caps, inner_source_ref, inner_target_ref, inner_gain_ref
    ).T


def stamp_kernel(
    per_owner,
    facts_ref,
    facts_other,
    table_ref,
    table_other,
    source_ref,
    source_other,
    target_ref,
    target_other,
    gain_ref,
    gain_other,
    target_out,
    gain_out,
    near_ref,
    right_ref,
    row_hot_ref,
    place_ref,
    offset_hot_ref,
):
    own_count, elements = source_ref.shape
    stamp_count = 2 * own_count
    block_count = table_ref.shape[1]
    half = block_count // 2
    group = NEWTON * GROUP
    later = lax.axis_index("sub") == 1
    tables = []
    for ref in (table_ref, table_other):
        field = jnp.where(later, ref[0] + ref[1], ref[0])
        update = jnp.where(later, ref[2], ref[1]).astype(BF16).astype(F32)
        tables.append(jnp.concatenate([field, update], axis=1))
    tables = jnp.concatenate(tables, axis=0)

    facts = jnp.concatenate([facts_ref[...], facts_other[...]], axis=1).astype(F32)
    block_row, owner_row, offset_row = facts[0:1], facts[1:2], facts[2:3]
    mine = iota((1, stamp_count), 1) < own_count
    block = row_to_column(jnp.where(mine, block_row, block_row + block_count))
    owner = row_to_column(owner_row)
    offset = row_to_column(offset_row)
    upper = jnp.where(offset < half, 0, 1)
    row_hot = iota(row_hot_ref.shape, 1).astype(F32) == owner * half + offset - half * upper.astype(F32)
    row_hot_ref[...] = row_hot.astype(F32).astype(BF16)
    shape = (stamp_count, stamp_count)
    row, column = iota(shape, 0), iota(shape, 1)
    earlier = (owner == owner_row) & (row < column) & ((row < own_count) == (column < own_count))
    rank_row = jnp.sum(jnp.where(earlier, 1.0, 0.0), axis=0, keepdims=True)
    rank_row = jnp.where(mine, rank_row, rank_row + per_owner)
    slot_row = owner_row * (2 * per_owner) + rank_row
    place = iota(place_ref.shape, 0).astype(F32) == slot_row
    place_ref[...] = place.astype(F32).astype(BF16)
    offset_hot = iota(offset_hot_ref.shape, 1).astype(F32) == offset
    offset_hot_ref[...] = offset_hot.astype(F32).astype(BF16)

    block_hot = iota((stamp_count, 2 * block_count), 1).astype(F32) == block
    block_hot = block_hot.astype(F32).astype(BF16)
    local = sum(dot(block_hot, p, NN) for p in split(tables, 3))
    for n, (sources, targets, gains) in enumerate(
        ((source_ref, target_ref, gain_ref), (source_other, target_other, gain_other))
    ):
        held = slice(n * own_count, (n + 1) * own_count)
        gain_out[held, :] = -gains[...]
        near = local[held]
        for at in range(0, elements, LANES):
            lanes = slice(at, at + LANES)
            source = sources[:, lanes]
            near_ref[held, lanes] = pick(near, source)
            moved = pick(near, source + BS).astype(BF16)
            target = targets[:, lanes]
            target_out[held, lanes] = (target + upper[held] * BS).astype(F32).astype(BF16)
            low = digits(target)[1]
            for start in range(0, own_count, group):
                rows = slice(start, start + group)
                first = DIGIT * (n * own_count + start)
                right_ref[first : first + DIGIT * group, lanes] = hot_rows(low[rows], [moved[rows]])


def couple_kernel(
    fields_ref,
    target_ref,
    gain_ref,
    near_ref,
    right_ref,
    row_hot_ref,
    place_ref,
    offset_hot_ref,
    send_ref,
    left_ref,
    product_ref,
):
    stamp_count, elements = target_ref.shape
    group = NEWTON * GROUP
    rows_of = DIGIT * group
    remote = dot(row_hot_ref[...], fields_ref[...], NN)
    for start in range(0, stamp_count, group):
        rows = slice(start, start + group)
        held = slice(DIGIT * start, DIGIT * start + rows_of)
        for at in range(0, elements, LANES):
            lanes = slice(at, at + LANES)
            target = target_ref[rows, lanes].astype(F32).astype(jnp.int32)
            high = digits(target & (BS - 1))[0]
            far = pick(remote[rows], target)
            weight = conductance(gain_ref[rows, lanes], near_ref[rows, lanes], far)
            left_ref[held, lanes] = hot_rows(high, [weight.astype(BF16)])
    same = same_block((rows_of, rows_of), group)
    for start in range(0, DIGIT * stamp_count, rows_of):
        held = slice(start, start + rows_of)
        product = dot(left_ref[held, :], right_ref[held, :], NT)
        product_ref[held, :] = jnp.where(same, product, 0.0).astype(BF16)
    shape = (rows_of, LANES)
    node = iota(shape, 1) - BS
    nodes = (node >= 0) & (node % DIGIT == iota(shape, 0) // group)
    wide = dot(product_ref[...], nodes.astype(F32).astype(BF16), NN)
    high_lane = (iota((group, LANES), 1) - BS) // DIGIT
    images = []
    for start in range(0, DIGIT * stamp_count, rows_of):
        total = jnp.zeros((group, LANES), F32)
        for h in range(DIGIT):
            slab = wide[start + h * group : start + (h + 1) * group]
            total = total + jnp.where(high_lane == h, slab, 0.0)
        images.append(total)
    images = jnp.concatenate(images, axis=0)
    messages = images.astype(BF16) + offset_hot_ref[...]
    send_ref[...] = dot(place_ref[...], messages, NN).astype(BF16)


def pack_kernel(precond_ref, packed_ref):
    for g in range(packed_ref.shape[0]):
        parts = [precond_ref[i] for i in range(g, BS, packed_ref.shape[0])]
        packed_ref[g] = jnp.concatenate(parts, axis=0).T


def finish_kernel(row_count, images_ref, inner_ref, packed_ref, out_ref):
    received = images_ref[...]
    block_count = inner_ref.shape[1]
    parts = LANES // block_count
    step = iota(received.shape, 0) // row_count % NEWTON
    totals = []
    for t in range(NEWTON):
        mine = jnp.where(step == t, received.astype(F32), 0.0).astype(BF16)
        couple = dot(received, mine, TN)[BS:, :block_count]
        total = inner_ref[t * BS : (t + 1) * BS, :] + couple
        totals.append(jnp.concatenate([total] * parts, axis=1))
    rows = [[] for _ in range(NEWTON)]
    for g in range(packed_ref.shape[0]):
        packed = packed_ref[g]
        for t in range(NEWTON):
            rows[t].append(jnp.sum(packed * totals[t], axis=0, keepdims=True))
    for t in range(NEWTON):
        wide = jnp.concatenate(rows[t], axis=0).T
        out_ref[t] = jnp.concatenate(
            [wide[k * block_count : (k + 1) * block_count] for k in range(parts)], axis=1
        )


def call(kernel, out_shape, args, cost, scratch=()):
    spec = pl.BlockSpec(memory_space=pltpu.VMEM)
    several = isinstance(out_shape, (list, tuple))
    return pl.pallas_call(
        kernel,
        out_shape=out_shape,
        in_specs=[spec] * len(args),
        out_specs=[spec] * len(out_shape) if several else spec,
        scratch_shapes=list(scratch),
        compiler_params=pltpu.CompilerParams(vmem_limit_bytes=24 * 2**20),
        cost_estimate=pl.CostEstimate(flops=cost[0], bytes_accessed=cost[1], transcendentals=0),
    )(*args)


def exchange(rows, devices):
    shaped = rows.reshape((devices, rows.shape[0] // devices, rows.shape[1]))
    out = lax.all_to_all(shaped, AXES, split_axis=0, concat_axis=0, tiled=True)
    return out.reshape(rows.shape)


def per_device(
    voltages,
    newton_steps,
    cap_diag,
    preconditioner,
    couple_block,
    couple_owner,
    couple_offset,
    couple_source,
    couple_target,
    couple_gain,
    inner_source,
    inner_target,
    inner_gain,
):
    devices = lax.axis_size(AXES)
    stamp_count, elements = couple_source.shape
    block_count = voltages.shape[1]
    per_owner = max(2, 2 * stamp_count // devices)
    row_count = devices * per_owner * NEWTON
    like = jax.ShapeDtypeStruct
    swap = lambda array: lax.ppermute(array, "sub", [(0, 1), (1, 0)])
    table = jnp.concatenate([voltages.T[None], newton_steps.transpose(0, 2, 1)], axis=0)
    send = call(
        prepare_kernel, like((devices * block_count // 2, LANES), BF16), (table,), (2 * 10**10, 10**6)
    )
    fields = exchange(send, devices)
    inner = call(
        inner_kernel,
        like((NEWTON * BS, block_count), F32),
        (table, cap_diag.T, inner_source, inner_target, inner_gain),
        (4 * 10**9, 10**6),
    )
    packed = call(
        pack_kernel,
        like((BS * block_count // LANES, BS, LANES), F32),
        (preconditioner.transpose(0, 2, 1),),
        (10**8, 10**6),
    )
    facts = [fact.reshape(1, stamp_count) for fact in (couple_block, couple_owner, couple_offset)]
    wanted = (jnp.concatenate(facts, axis=0), table, couple_source, couple_target, couple_gain)
    pairs = [half for array in wanted for half in (array, swap(array))]
    both = 2 * stamp_count
    prepared = call(
        functools.partial(stamp_kernel, per_owner),
        [
            like((both, elements), BF16),
            like((both, elements), couple_gain.dtype),
            like((both, elements), F32),
            like((DIGIT * both, elements), BF16),
            like((both, devices * block_count // 2), BF16),
            like((row_count, both), BF16),
            like((both, LANES), BF16),
        ],
        pairs,
        (4 * 10**8, 10**6),
    )
    images = call(
        couple_kernel,
        like((row_count, LANES), BF16),
        (fields, *prepared),
        (4 * 10**9, 10**6),
        [
            pltpu.VMEM((DIGIT * both, elements), BF16),
            pltpu.VMEM((DIGIT * both, DIGIT * NEWTON * GROUP), BF16),
        ],
    )
    received = exchange(images, devices)
    out = call(
        functools.partial(finish_kernel, 2 * per_owner),
        like((NEWTON, block_count, BS), F32),
        (received, inner, packed),
        (10**8, 10**6),
    )
    return out.transpose(0, 2, 1)


def solution(mesh):
    in_specs = (
        P(None, AXES),
        P(None, None, AXES),
        P(None, AXES),
        P(None, None, AXES),
        P(AXES),
        P(AXES, None),
        P(AXES),
        P(AXES, None),
        P(AXES, None),
        P(AXES, None),
        P(AXES, None),
        P(AXES, None),
        P(AXES, None),
    )
    out_specs = P(None, None, AXES)
    return jax.shard_map(
        per_device, mesh=mesh, in_specs=in_specs, out_specs=out_specs, check_vma=False
    )
```

```python
import functools

import jax
import jax.numpy as jnp
from jax import lax
from jax.experimental import pallas as pl
from jax.experimental.pallas import tpu as pltpu
from jax.sharding import PartitionSpec as P

BS = 64
NEWTON = 2
LANES = 128
GROUP = 16
DIGIT = 8
AXES = ("dom", "sub")
NT = (((1,), (1,)), ((), ()))
TN = (((0,), (0,)), ((), ()))
NN = (((1,), (0,)), ((), ()))
F32 = jnp.float32
BF16 = jnp.bfloat16


def iota(shape, axis):
    return lax.broadcasted_iota(jnp.int32, shape, axis)


def dot(first, second, numbers):
    return lax.dot_general(first, second, numbers, preferred_element_type=F32)


def pick(table, index):
    return jnp.concatenate(
        [
            jnp.take_along_axis(table[r : r + 8], index[r : r + 8], axis=1)
            for r in range(0, table.shape[0], 8)
        ],
        axis=0,
    )


def conductance(gain, first, second):
    drop = first - second
    return gain / (1.0 + drop * drop)


def digits(index):
    high = lax.shift_right_logical(index, 3)
    return high.astype(F32).astype(BF16), (index - high * DIGIT).astype(F32).astype(BF16)


def hot_rows(digit, values):
    zero = jnp.zeros_like(values[0])
    masks = [digit == jnp.asarray(d, BF16) for d in range(DIGIT)]
    return jnp.concatenate([jnp.where(m, v, zero) for v in values for m in masks], axis=0)


def same_block(shape, group):
    return (iota(shape, 0) % group) == (iota(shape, 1) % group)


def gather_nodes(spread):
    shape = (NEWTON * DIGIT * GROUP, LANES)
    column, lane = iota(shape, 0), iota(shape, 1)
    low = (column // GROUP) % DIGIT
    step = column // (GROUP * DIGIT)
    keep = low == lane % DIGIT
    if spread:
        keep = keep & (step == lane // BS)
    return keep.astype(F32).astype(BF16)


def fold_rows(wide):
    lane = iota((GROUP, LANES), 1) // DIGIT
    total = jnp.zeros((GROUP, LANES), F32)
    for s in range(NEWTON * DIGIT):
        total = total + jnp.where(lane == s, wide[s * GROUP : (s + 1) * GROUP], 0.0)
    return total


def split(value, parts):
    pieces = []
    for _ in range(parts):
        piece = value.astype(BF16)
        pieces.append(piece)
        value = value - piece.astype(F32)
    return pieces


def fields_of(table_ref):
    first = table_ref[0]
    return jnp.concatenate([first, first + table_ref[1]], axis=1)


def prepare_kernel(table_ref, send_ref):
    block_count = table_ref.shape[1]
    half = block_count // 2
    first = table_ref[0]
    packed = [
        jnp.concatenate([field[:half], field[half:]], axis=1).astype(BF16)
        for field in (first, first + table_ref[1])
    ]
    for d in range(send_ref.shape[0] // half):
        send_ref[pl.ds(d * half, half), :] = packed[d % NEWTON]


def inner_images(volt_rows, update_rows, cap_rows, source_ref, target_ref, gain_ref):
    block_count, elements = source_ref.shape
    nodes_any, nodes_step = gather_nodes(False), gather_nodes(True)
    images = []
    for start in range(0, block_count, GROUP):
        rows = slice(start, start + GROUP)
        volts, updates = volt_rows[rows], update_rows[rows]
        acc_ones = jnp.zeros((NEWTON * DIGIT * GROUP, DIGIT * GROUP), F32)
        acc = jnp.zeros((NEWTON * DIGIT * GROUP, NEWTON * DIGIT * GROUP), F32)
        for at in range(0, elements, LANES):
            lanes = slice(at, at + LANES)
            source, target = source_ref[rows, lanes], target_ref[rows, lanes]
            gain = jnp.where(source == target, 0.0, gain_ref[rows, lanes])
            weights, source_updates, target_updates = [], [], []
            for t in range(NEWTON):
                here, there = source + t * BS, target + t * BS
                weights.append(
                    conductance(gain, pick(volts, here), pick(volts, there)).astype(BF16)
                )
                source_updates.append(pick(updates, here).astype(BF16))
                target_updates.append(pick(updates, there).astype(BF16))
            ones = jnp.ones((GROUP, LANES), BF16)
            left, right, right_ones = [], [], []
            for index, others in ((source, target_updates), (target, source_updates)):
                high, low = digits(index)
                left.append(hot_rows(high, weights))
                right_ones.append(hot_rows(low, [ones]))
                right.append(hot_rows(low, others))
            left = jnp.concatenate(left, axis=1)
            acc_ones = acc_ones + dot(left, jnp.concatenate(right_ones, axis=1), NT)
            acc = acc + dot(left, jnp.concatenate(right, axis=1), NT)
        acc = jnp.where(same_block(acc.shape, GROUP), acc, 0.0)
        acc_ones = jnp.where(same_block(acc_ones.shape, GROUP), acc_ones, 0.0)
        diagonal = fold_rows(
            sum(dot(p, nodes_any[: DIGIT * GROUP], NN) for p in split(acc_ones, 2))
        )
        others = fold_rows(sum(dot(p, nodes_step, NN) for p in split(acc, 2)))
        diagonal = (diagonal + cap_rows[rows]).astype(BF16).astype(F32)
        images.append(diagonal * updates - others)
    return jnp.concatenate(images, axis=0)


def row_to_column(row):
    count = row.shape[1]
    shape = (count, count)
    return jnp.sum(jnp.where(iota(shape, 0) == iota(shape, 1), row, 0), axis=1, keepdims=True)


def inner_kernel(
    table_ref,
    cap_ref,
    inner_source_ref,
    inner_target_ref,
    inner_gain_ref,
    inner_ref,
):
    updates = jnp.concatenate([table_ref[1], table_ref[2]], axis=1).astype(BF16).astype(F32)
    caps = jnp.concatenate([cap_ref[...], cap_ref[...]], axis=1)
    inner_ref[...] = inner_images(
        fields_of(table_ref), updates, caps, inner_source_ref, inner_target_ref, inner_gain_ref
    ).T


def stamp_kernel(
    per_owner,
    facts_ref,
    facts_other,
    table_ref,
    table_other,
    source_ref,
    source_other,
    target_ref,
    target_other,
    gain_ref,
    gain_other,
    target_out,
    gain_out,
    near_ref,
    right_ref,
    moved_ref,
    row_hot_ref,
    place_ref,
    offset_hot_ref,
):
    own_count, elements = source_ref.shape
    stamp_count = 2 * own_count
    block_count = table_ref.shape[1]
    half = block_count // 2
    group = NEWTON * GROUP
    later = lax.axis_index("sub") == 1
    tables = []
    for ref in (table_ref, table_other):
        field = jnp.where(later, ref[0] + ref[1], ref[0])
        update = jnp.where(later, ref[2], ref[1]).astype(BF16).astype(F32)
        tables.append(jnp.concatenate([field, update], axis=1))
    tables = jnp.concatenate(tables, axis=0)

    facts = jnp.concatenate([facts_ref[...], facts_other[...]], axis=1).astype(F32)
    block_row, owner_row, offset_row = facts[0:1], facts[1:2], facts[2:3]
    mine = iota((1, stamp_count), 1) < own_count
    block = row_to_column(jnp.where(mine, block_row, block_row + block_count))
    owner = row_to_column(owner_row)
    offset = row_to_column(offset_row)
    upper = jnp.where(offset < half, 0, 1)
    row_hot = iota(row_hot_ref.shape, 1).astype(F32) == owner * half + offset - half * upper.astype(F32)
    row_hot_ref[...] = row_hot.astype(F32).astype(BF16)
    shape = (stamp_count, stamp_count)
    row, column = iota(shape, 0), iota(shape, 1)
    earlier = (owner == owner_row) & (row < column) & ((row < own_count) == (column < own_count))
    rank_row = jnp.sum(jnp.where(earlier, 1.0, 0.0), axis=0, keepdims=True)
    rank_row = jnp.where(mine, rank_row, rank_row + per_owner)
    slot_row = owner_row * (2 * per_owner) + rank_row
    place = iota(place_ref.shape, 0).astype(F32) == slot_row
    place_ref[...] = place.astype(F32).astype(BF16)
    offset_hot = iota(offset_hot_ref.shape, 1).astype(F32) == offset
    offset_hot_ref[...] = offset_hot.astype(F32).astype(BF16)

    block_hot = iota((stamp_count, 2 * block_count), 1).astype(F32) == block
    block_hot = block_hot.astype(F32).astype(BF16)
    local = sum(dot(block_hot, p, NN) for p in split(tables, 3))
    for n, (sources, targets, gains) in enumerate(
        ((source_ref, target_ref, gain_ref), (source_other, target_other, gain_other))
    ):
        held = slice(n * own_count, (n + 1) * own_count)
        gain_out[held, :] = -gains[...]
        near = local[held]
        for at in range(0, elements, LANES):
            lanes = slice(at, at + LANES)
            source = sources[:, lanes]
            near_ref[held, lanes] = pick(near, source)
            moved = pick(near, source + BS).astype(BF16)
            target = targets[:, lanes]
            target_out[held, lanes] = (target + upper[held] * BS).astype(F32).astype(BF16)
            if n > 0:
                moved_ref[:, lanes] = moved
                continue
            low = digits(target)[1]
            for start in range(0, own_count, group):
                rows = slice(start, start + group)
                held_rows = slice(DIGIT * start, DIGIT * (start + group))
                right_ref[held_rows, lanes] = hot_rows(low[rows], [moved[rows]])


def couple_kernel(
    fields_ref,
    target_ref,
    gain_ref,
    near_ref,
    right_ref,
    moved_ref,
    row_hot_ref,
    place_ref,
    offset_hot_ref,
    send_ref,
    left_ref,
    late_ref,
    product_ref,
):
    stamp_count, elements = target_ref.shape
    group = NEWTON * GROUP
    rows_of = DIGIT * group
    early = right_ref.shape[0] // DIGIT
    remote = dot(row_hot_ref[...], fields_ref[...], NN)
    for start in range(0, stamp_count, group):
        rows = slice(start, start + group)
        held = slice(DIGIT * start, DIGIT * start + rows_of)
        for at in range(0, elements, LANES):
            lanes = slice(at, at + LANES)
            target = target_ref[rows, lanes].astype(F32).astype(jnp.int32)
            high, low = digits(target & (BS - 1))
            if start >= early:
                moved = moved_ref[start - early : start - early + group, lanes]
                late = slice(held.start - DIGIT * early, held.stop - DIGIT * early)
                late_ref[late, lanes] = hot_rows(low, [moved])
            far = pick(remote[rows], target)
            weight = conductance(gain_ref[rows, lanes], near_ref[rows, lanes], far)
            left_ref[held, lanes] = hot_rows(high, [weight.astype(BF16)])
    same = same_block((rows_of, rows_of), group)
    for start in range(0, DIGIT * stamp_count, rows_of):
        held = slice(start, start + rows_of)
        if start < DIGIT * early:
            right = right_ref[held, :]
        else:
            right = late_ref[start - DIGIT * early : start - DIGIT * early + rows_of, :]
        product = dot(left_ref[held, :], right, NT)
        product_ref[held, :] = jnp.where(same, product, 0.0).astype(BF16)
    shape = (rows_of, LANES)
    node = iota(shape, 1) - BS
    nodes = (node >= 0) & (node % DIGIT == iota(shape, 0) // group)
    wide = dot(product_ref[...], nodes.astype(F32).astype(BF16), NN)
    high_lane = (iota((group, LANES), 1) - BS) // DIGIT
    images = []
    for start in range(0, DIGIT * stamp_count, rows_of):
        total = jnp.zeros((group, LANES), F32)
        for h in range(DIGIT):
            slab = wide[start + h * group : start + (h + 1) * group]
            total = total + jnp.where(high_lane == h, slab, 0.0)
        images.append(total)
    images = jnp.concatenate(images, axis=0)
    messages = images.astype(BF16) + offset_hot_ref[...]
    send_ref[...] = dot(place_ref[...], messages, NN).astype(BF16)


def pack_kernel(precond_ref, packed_ref):
    for g in range(packed_ref.shape[0]):
        parts = [precond_ref[i] for i in range(g, BS, packed_ref.shape[0])]
        packed_ref[g] = jnp.concatenate(parts, axis=0).T


def finish_kernel(row_count, images_ref, inner_ref, packed_ref, out_ref):
    received = images_ref[...]
    block_count = inner_ref.shape[1]
    parts = LANES // block_count
    step = iota(received.shape, 0) // row_count % NEWTON
    totals = []
    for t in range(NEWTON):
        mine = jnp.where(step == t, received.astype(F32), 0.0).astype(BF16)
        couple = dot(received, mine, TN)[BS:, :block_count]
        total = inner_ref[t * BS : (t + 1) * BS, :] + couple
        totals.append(jnp.concatenate([total] * parts, axis=1))
    rows = [[] for _ in range(NEWTON)]
    for g in range(packed_ref.shape[0]):
        packed = packed_ref[g]
        for t in range(NEWTON):
            rows[t].append(jnp.sum(packed * totals[t], axis=0, keepdims=True))
    for t in range(NEWTON):
        wide = jnp.concatenate(rows[t], axis=0).T
        out_ref[t] = jnp.concatenate(
            [wide[k * block_count : (k + 1) * block_count] for k in range(parts)], axis=1
        )


def call(kernel, out_shape, args, cost, scratch=()):
    spec = pl.BlockSpec(memory_space=pltpu.VMEM)
    several = isinstance(out_shape, (list, tuple))
    return pl.pallas_call(
        kernel,
        out_shape=out_shape,
        in_specs=[spec] * len(args),
        out_specs=[spec] * len(out_shape) if several else spec,
        scratch_shapes=list(scratch),
        compiler_params=pltpu.CompilerParams(vmem_limit_bytes=24 * 2**20),
        cost_estimate=pl.CostEstimate(flops=cost[0], bytes_accessed=cost[1], transcendentals=0),
    )(*args)


def exchange(rows, devices):
    shaped = rows.reshape((devices, rows.shape[0] // devices, rows.shape[1]))
    out = lax.all_to_all(shaped, AXES, split_axis=0, concat_axis=0, tiled=True)
    return out.reshape(rows.shape)


def per_device(
    voltages,
    newton_steps,
    cap_diag,
    preconditioner,
    couple_block,
    couple_owner,
    couple_offset,
    couple_source,
    couple_target,
    couple_gain,
    inner_source,
    inner_target,
    inner_gain,
):
    devices = lax.axis_size(AXES)
    stamp_count, elements = couple_source.shape
    block_count = voltages.shape[1]
    per_owner = max(2, 2 * stamp_count // devices)
    row_count = devices * per_owner * NEWTON
    like = jax.ShapeDtypeStruct
    swap = lambda array: lax.ppermute(array, "sub", [(0, 1), (1, 0)])
    table = jnp.concatenate([voltages.T[None], newton_steps.transpose(0, 2, 1)], axis=0)
    send = call(
        prepare_kernel, like((devices * block_count // 2, LANES), BF16), (table,), (2 * 10**10, 10**6)
    )
    facts = [fact.reshape(1, stamp_count) for fact in (couple_block, couple_owner, couple_offset)]
    send, facts = lax.optimization_barrier((send, jnp.concatenate(facts, axis=0)))
    fields = exchange(send, devices)
    inner = call(
        inner_kernel,
        like((NEWTON * BS, block_count), F32),
        (table, cap_diag.T, inner_source, inner_target, inner_gain),
        (10**9, 10**6),
    )
    packed = call(
        pack_kernel,
        like((BS * block_count // LANES, BS, LANES), F32),
        (preconditioner.transpose(0, 2, 1),),
        (10**8, 10**6),
    )
    wanted = (facts, table, couple_source, couple_target, couple_gain)
    pairs = [half for array in wanted for half in (array, swap(array))]
    both = 2 * stamp_count
    prepared = call(
        functools.partial(stamp_kernel, per_owner),
        [
            like((both, elements), BF16),
            like((both, elements), F32),
            like((both, elements), F32),
            like((DIGIT * stamp_count, elements), BF16),
            like((stamp_count, elements), BF16),
            like((both, devices * block_count // 2), BF16),
            like((row_count, both), BF16),
            like((both, LANES), BF16),
        ],
        pairs,
        (10**8, 10**6),
    )
    fields, inner, packed = lax.optimization_barrier((fields, inner, packed))
    images = call(
        couple_kernel,
        like((row_count, LANES), BF16),
        (fields, *prepared),
        (4 * 10**9, 10**6),
        [
            pltpu.VMEM((DIGIT * both, elements), BF16),
            pltpu.VMEM((DIGIT * stamp_count, elements), BF16),
            pltpu.VMEM((DIGIT * both, DIGIT * NEWTON * GROUP), BF16),
        ],
    )
    received = exchange(images, devices)
    out = call(
        functools.partial(finish_kernel, 2 * per_owner),
        like((NEWTON, block_count, BS), F32),
        (received, inner, packed),
        (10**8, 10**6),
    )
    return out.transpose(0, 2, 1)


def solution(mesh):
    in_specs = (
        P(None, AXES),
        P(None, None, AXES),
        P(None, AXES),
        P(None, None, AXES),
        P(AXES),
        P(AXES, None),
        P(AXES),
        P(AXES, None),
        P(AXES, None),
        P(AXES, None),
        P(AXES, None),
        P(AXES, None),
        P(AXES, None),
    )
    out_specs = P(None, None, AXES)
    return jax.shard_map(
        per_device, mesh=mesh, in_specs=in_specs, out_specs=out_specs, check_vma=False
    )
```

```python
import functools

import jax
import jax.numpy as jnp
from jax import lax
from jax.experimental import pallas as pl
from jax.experimental.pallas import tpu as pltpu
from jax.sharding import PartitionSpec as P

BS = 64
NEWTON = 2
LANES = 128
GROUP = 16
DIGIT = 8
AXES = ("dom", "sub")
NT = (((1,), (1,)), ((), ()))
TN = (((0,), (0,)), ((), ()))
NN = (((1,), (0,)), ((), ()))
F32 = jnp.float32
BF16 = jnp.bfloat16


def iota(shape, axis):
    return lax.broadcasted_iota(jnp.int32, shape, axis)


def dot(first, second, numbers):
    return lax.dot_general(first, second, numbers, preferred_element_type=F32)


def pick(table, index):
    return jnp.concatenate(
        [
            jnp.take_along_axis(table[r : r + 8], index[r : r + 8], axis=1)
            for r in range(0, table.shape[0], 8)
        ],
        axis=0,
    )


def conductance(gain, first, second):
    drop = first - second
    return gain / (1.0 + drop * drop)


def digits(index):
    high = lax.shift_right_logical(index, 3)
    return high.astype(F32).astype(BF16), (index - high * DIGIT).astype(F32).astype(BF16)


def hot_rows(digit, values):
    zero = jnp.zeros_like(values[0])
    masks = [digit == jnp.asarray(d, BF16) for d in range(DIGIT)]
    return jnp.concatenate([jnp.where(m, v, zero) for v in values for m in masks], axis=0)


def same_block(shape, group):
    return (iota(shape, 0) % group) == (iota(shape, 1) % group)


def gather_nodes(spread):
    shape = (NEWTON * DIGIT * GROUP, LANES)
    column, lane = iota(shape, 0), iota(shape, 1)
    low = (column // GROUP) % DIGIT
    step = column // (GROUP * DIGIT)
    keep = low == lane % DIGIT
    if spread:
        keep = keep & (step == lane // BS)
    return keep.astype(F32).astype(BF16)


def fold_rows(wide):
    lane = iota((GROUP, LANES), 1) // DIGIT
    total = jnp.zeros((GROUP, LANES), F32)
    for s in range(NEWTON * DIGIT):
        total = total + jnp.where(lane == s, wide[s * GROUP : (s + 1) * GROUP], 0.0)
    return total


def split(value, parts):
    pieces = []
    for _ in range(parts):
        piece = value.astype(BF16)
        pieces.append(piece)
        value = value - piece.astype(F32)
    return pieces


def fields_of(table_ref):
    first = table_ref[0]
    return jnp.concatenate([first, first + table_ref[1]], axis=1)


def prepare_kernel(table_ref, send_ref):
    block_count = table_ref.shape[1]
    half = block_count // 2
    first = table_ref[0]
    packed = [
        jnp.concatenate([field[:half], field[half:]], axis=1).astype(BF16)
        for field in (first, first + table_ref[1])
    ]
    for d in range(send_ref.shape[0] // half):
        send_ref[pl.ds(d * half, half), :] = packed[d % NEWTON]


def inner_images(volt_rows, update_rows, cap_rows, source_ref, target_ref, gain_ref):
    block_count, elements = source_ref.shape
    nodes_any, nodes_step = gather_nodes(False), gather_nodes(True)
    images = []
    for start in range(0, block_count, GROUP):
        rows = slice(start, start + GROUP)
        volts, updates = volt_rows[rows], update_rows[rows]
        acc_ones = jnp.zeros((NEWTON * DIGIT * GROUP, DIGIT * GROUP), F32)
        acc = jnp.zeros((NEWTON * DIGIT * GROUP, NEWTON * DIGIT * GROUP), F32)
        for at in range(0, elements, LANES):
            lanes = slice(at, at + LANES)
            source, target = source_ref[rows, lanes], target_ref[rows, lanes]
            gain = jnp.where(source == target, 0.0, gain_ref[rows, lanes])
            weights, source_updates, target_updates = [], [], []
            for t in range(NEWTON):
                here, there = source + t * BS, target + t * BS
                weights.append(
                    conductance(gain, pick(volts, here), pick(volts, there)).astype(BF16)
                )
                source_updates.append(pick(updates, here).astype(BF16))
                target_updates.append(pick(updates, there).astype(BF16))
            ones = jnp.ones((GROUP, LANES), BF16)
            left, right, right_ones = [], [], []
            for index, others in ((source, target_updates), (target, source_updates)):
                high, low = digits(index)
                left.append(hot_rows(high, weights))
                right_ones.append(hot_rows(low, [ones]))
                right.append(hot_rows(low, others))
            left = jnp.concatenate(left, axis=1)
            acc_ones = acc_ones + dot(left, jnp.concatenate(right_ones, axis=1), NT)
            acc = acc + dot(left, jnp.concatenate(right, axis=1), NT)
        acc = jnp.where(same_block(acc.shape, GROUP), acc, 0.0)
        acc_ones = jnp.where(same_block(acc_ones.shape, GROUP), acc_ones, 0.0)
        diagonal = fold_rows(
            sum(dot(p, nodes_any[: DIGIT * GROUP], NN) for p in split(acc_ones, 2))
        )
        others = fold_rows(sum(dot(p, nodes_step, NN) for p in split(acc, 2)))
        diagonal = (diagonal + cap_rows[rows]).astype(BF16).astype(F32)
        images.append(diagonal * updates - others)
    return jnp.concatenate(images, axis=0)


def row_to_column(row):
    count = row.shape[1]
    shape = (count, count)
    return jnp.sum(jnp.where(iota(shape, 0) == iota(shape, 1), row, 0), axis=1, keepdims=True)


def inner_kernel(
    table_ref,
    cap_ref,
    inner_source_ref,
    inner_target_ref,
    inner_gain_ref,
    precond_ref,
    inner_ref,
    packed_ref,
):
    for g in range(packed_ref.shape[0]):
        parts = [precond_ref[i] for i in range(g, BS, packed_ref.shape[0])]
        packed_ref[g] = jnp.concatenate(parts, axis=0).T
    updates = jnp.concatenate([table_ref[1], table_ref[2]], axis=1).astype(BF16).astype(F32)
    caps = jnp.concatenate([cap_ref[...], cap_ref[...]], axis=1)
    inner_ref[...] = inner_images(
        fields_of(table_ref), updates, caps, inner_source_ref, inner_target_ref, inner_gain_ref
    ).T


def stamp_kernel(
    per_owner,
    facts_ref,
    facts_other,
    table_ref,
    table_other,
    source_ref,
    source_other,
    target_ref,
    target_other,
    gain_ref,
    gain_other,
    target_out,
    gain_out,
    near_ref,
    moved_ref,
    row_hot_ref,
    place_ref,
    offset_hot_ref,
):
    own_count, elements = source_ref.shape
    stamp_count = 2 * own_count
    block_count = table_ref.shape[1]
    half = block_count // 2
    later = lax.axis_index("sub") == 1
    tables = []
    for ref in (table_ref, table_other):
        field = jnp.where(later, ref[0] + ref[1], ref[0])
        update = jnp.where(later, ref[2], ref[1]).astype(BF16).astype(F32)
        tables.append(jnp.concatenate([field, update], axis=1))
    tables = jnp.concatenate(tables, axis=0)

    facts = jnp.concatenate([facts_ref[...], facts_other[...]], axis=1).astype(F32)
    block_row, owner_row, offset_row = facts[0:1], facts[1:2], facts[2:3]
    mine = iota((1, stamp_count), 1) < own_count
    block = row_to_column(jnp.where(mine, block_row, block_row + block_count))
    owner = row_to_column(owner_row)
    offset = row_to_column(offset_row)
    upper = jnp.where(offset < half, 0, 1)
    row_hot = iota(row_hot_ref.shape, 1).astype(F32) == owner * half + offset - half * upper.astype(F32)
    row_hot_ref[...] = row_hot.astype(F32).astype(BF16)
    shape = (stamp_count, stamp_count)
    row, column = iota(shape, 0), iota(shape, 1)
    earlier = (owner == owner_row) & (row < column) & ((row < own_count) == (column < own_count))
    rank_row = jnp.sum(jnp.where(earlier, 1.0, 0.0), axis=0, keepdims=True)
    rank_row = jnp.where(mine, rank_row, rank_row + per_owner)
    slot_row = owner_row * (2 * per_owner) + rank_row
    place = iota(place_ref.shape, 0).astype(F32) == slot_row
    place_ref[...] = place.astype(F32).astype(BF16)
    offset_hot = iota(offset_hot_ref.shape, 1).astype(F32) == offset
    offset_hot_ref[...] = offset_hot.astype(F32).astype(BF16)

    block_hot = iota((stamp_count, 2 * block_count), 1).astype(F32) == block
    block_hot = block_hot.astype(F32).astype(BF16)
    local = sum(dot(block_hot, p, NN) for p in split(tables, 3))
    for n, (sources, targets, gains) in enumerate(
        ((source_ref, target_ref, gain_ref), (source_other, target_other, gain_other))
    ):
        held = slice(n * own_count, (n + 1) * own_count)
        gain_out[held, :] = -gains[...]
        near = local[held]
        for at in range(0, elements, LANES):
            lanes = slice(at, at + LANES)
            source = sources[:, lanes]
            near_ref[held, lanes] = pick(near, source)
            moved_ref[held, lanes] = pick(near, source + BS).astype(BF16)
            target = targets[:, lanes] + upper[held] * BS
            target_out[held, lanes] = target.astype(F32).astype(BF16)

def couple_kernel(
    fields_ref,
    target_ref,
    gain_ref,
    near_ref,
    moved_ref,
    row_hot_ref,
    place_ref,
    offset_hot_ref,
    send_ref,
    product_ref,
):
    stamp_count, elements = target_ref.shape
    group = NEWTON * GROUP
    rows_of = DIGIT * group
    same = same_block((rows_of, rows_of), group)
    remote = dot(row_hot_ref[...], fields_ref[...], NN)
    for start in range(0, stamp_count, group):
        rows = slice(start, start + group)
        held = slice(DIGIT * start, DIGIT * start + rows_of)
        left, right = [], []
        for at in range(0, elements, LANES):
            lanes = slice(at, at + LANES)
            target = target_ref[rows, lanes].astype(F32).astype(jnp.int32)
            high, low = digits(target & (BS - 1))
            far = pick(remote[rows], target)
            weight = conductance(gain_ref[rows, lanes], near_ref[rows, lanes], far)
            left.append(hot_rows(high, [weight.astype(BF16)]))
            right.append(hot_rows(low, [moved_ref[rows, lanes]]))
        product = dot(jnp.concatenate(left, axis=1), jnp.concatenate(right, axis=1), NT)
        product_ref[held, :] = jnp.where(same, product, 0.0).astype(BF16)
    shape = (rows_of, LANES)
    node = iota(shape, 1) - BS
    nodes = (node >= 0) & (node % DIGIT == iota(shape, 0) // group)
    wide = dot(product_ref[...], nodes.astype(F32).astype(BF16), NN)
    high_lane = (iota((group, LANES), 1) - BS) // DIGIT
    images = []
    for start in range(0, DIGIT * stamp_count, rows_of):
        total = jnp.zeros((group, LANES), F32)
        for h in range(DIGIT):
            slab = wide[start + h * group : start + (h + 1) * group]
            total = total + jnp.where(high_lane == h, slab, 0.0)
        images.append(total)
    images = jnp.concatenate(images, axis=0)
    messages = images.astype(BF16) + offset_hot_ref[...]
    send_ref[...] = dot(place_ref[...], messages, NN).astype(BF16)


def finish_kernel(row_count, images_ref, inner_ref, packed_ref, out_ref):
    received = images_ref[...]
    block_count = inner_ref.shape[1]
    parts = LANES // block_count
    step = iota(received.shape, 0) // row_count % NEWTON
    totals = []
    for t in range(NEWTON):
        mine = jnp.where(step == t, received.astype(F32), 0.0).astype(BF16)
        couple = dot(received, mine, TN)[BS:, :block_count]
        total = inner_ref[t * BS : (t + 1) * BS, :] + couple
        totals.append(jnp.concatenate([total] * parts, axis=1))
    rows = [[] for _ in range(NEWTON)]
    for g in range(packed_ref.shape[0]):
        packed = packed_ref[g]
        for t in range(NEWTON):
            rows[t].append(jnp.sum(packed * totals[t], axis=0, keepdims=True))
    for t in range(NEWTON):
        wide = jnp.concatenate(rows[t], axis=0).T
        out_ref[t] = jnp.concatenate(
            [wide[k * block_count : (k + 1) * block_count] for k in range(parts)], axis=1
        )


def call(kernel, out_shape, args, cost, scratch=()):
    spec = pl.BlockSpec(memory_space=pltpu.VMEM)
    several = isinstance(out_shape, (list, tuple))
    return pl.pallas_call(
        kernel,
        out_shape=out_shape,
        in_specs=[spec] * len(args),
        out_specs=[spec] * len(out_shape) if several else spec,
        scratch_shapes=list(scratch),
        compiler_params=pltpu.CompilerParams(vmem_limit_bytes=24 * 2**20),
        cost_estimate=pl.CostEstimate(flops=cost[0], bytes_accessed=cost[1], transcendentals=0),
    )(*args)


def exchange(rows, devices):
    shaped = rows.reshape((devices, rows.shape[0] // devices, rows.shape[1]))
    out = lax.all_to_all(shaped, AXES, split_axis=0, concat_axis=0, tiled=True)
    return out.reshape(rows.shape)


def per_device(
    voltages,
    newton_steps,
    cap_diag,
    preconditioner,
    couple_block,
    couple_owner,
    couple_offset,
    couple_source,
    couple_target,
    couple_gain,
    inner_source,
    inner_target,
    inner_gain,
):
    devices = lax.axis_size(AXES)
    stamp_count, elements = couple_source.shape
    block_count = voltages.shape[1]
    per_owner = max(2, 2 * stamp_count // devices)
    row_count = devices * per_owner * NEWTON
    like = jax.ShapeDtypeStruct
    swap = lambda array: lax.ppermute(array, "sub", [(0, 1), (1, 0)])
    table = jnp.concatenate([voltages.T[None], newton_steps.transpose(0, 2, 1)], axis=0)
    send = call(
        prepare_kernel, like((devices * block_count // 2, LANES), BF16), (table,), (2 * 10**10, 10**6)
    )
    facts = [fact.reshape(1, stamp_count) for fact in (couple_block, couple_owner, couple_offset)]
    send, facts = lax.optimization_barrier((send, jnp.concatenate(facts, axis=0)))
    fields = exchange(send, devices)
    inner, packed = call(
        inner_kernel,
        [
            like((NEWTON * BS, block_count), F32),
            like((BS * block_count // LANES, BS, LANES), F32),
        ],
        (
            table,
            cap_diag.T,
            inner_source,
            inner_target,
            inner_gain,
            preconditioner.transpose(0, 2, 1),
        ),
        (10**9, 10**6),
    )
    wanted = (facts, table, couple_source, couple_target, couple_gain)
    pairs = [half for array in wanted for half in (array, swap(array))]
    both = 2 * stamp_count
    prepared = call(
        functools.partial(stamp_kernel, per_owner),
        [
            like((both, elements), BF16),
            like((both, elements), F32),
            like((both, elements), F32),
            like((both, elements), BF16),
            like((both, devices * block_count // 2), BF16),
            like((row_count, both), BF16),
            like((both, LANES), BF16),
        ],
        pairs,
        (10**8, 10**6),
    )
    fields, inner, packed = lax.optimization_barrier((fields, inner, packed))
    images = call(
        couple_kernel,
        like((row_count, LANES), BF16),
        (fields, *prepared),
        (4 * 10**9, 10**6),
        [
            pltpu.VMEM((DIGIT * both, DIGIT * NEWTON * GROUP), BF16),
        ],
    )
    received = exchange(images, devices)
    out = call(
        functools.partial(finish_kernel, 2 * per_owner),
        like((NEWTON, block_count, BS), F32),
        (received, inner, packed),
        (10**8, 10**6),
    )
    return out.transpose(0, 2, 1)


def solution(mesh):
    in_specs = (
        P(None, AXES),
        P(None, None, AXES),
        P(None, AXES),
        P(None, None, AXES),
        P(AXES),
        P(AXES, None),
        P(AXES),
        P(AXES, None),
        P(AXES, None),
        P(AXES, None),
        P(AXES, None),
        P(AXES, None),
        P(AXES, None),
    )
    out_specs = P(None, None, AXES)
    return jax.shard_map(
        per_device, mesh=mesh, in_specs=in_specs, out_specs=out_specs, check_vma=False
    )
```

```python
import functools

import jax
import jax.numpy as jnp
from jax import lax
from jax.experimental import pallas as pl
from jax.experimental.pallas import tpu as pltpu
from jax.sharding import PartitionSpec as P

BS = 64
NEWTON = 2
LANES = 128
GROUP = 16
DIGIT = 8
AXES = ("dom", "sub")
NT = (((1,), (1,)), ((), ()))
TN = (((0,), (0,)), ((), ()))
NN = (((1,), (0,)), ((), ()))
F32 = jnp.float32
BF16 = jnp.bfloat16


def iota(shape, axis):
    return lax.broadcasted_iota(jnp.int32, shape, axis)


def dot(first, second, numbers):
    return lax.dot_general(first, second, numbers, preferred_element_type=F32)


def pick(table, index):
    return jnp.concatenate(
        [
            jnp.take_along_axis(table[r : r + 8], index[r : r + 8], axis=1)
            for r in range(0, table.shape[0], 8)
        ],
        axis=0,
    )


def conductance(gain, first, second):
    drop = first - second
    return gain / (1.0 + drop * drop)


def digits(index):
    high = lax.shift_right_logical(index, 3)
    return high.astype(F32).astype(BF16), (index - high * DIGIT).astype(F32).astype(BF16)


def hot_rows(digit, values):
    zero = jnp.zeros_like(values[0])
    masks = [digit == jnp.asarray(d, BF16) for d in range(DIGIT)]
    return jnp.concatenate([jnp.where(m, v, zero) for v in values for m in masks], axis=0)


def same_block(shape, group):
    return (iota(shape, 0) % group) == (iota(shape, 1) % group)


def gather_nodes(spread):
    shape = (NEWTON * DIGIT * GROUP, LANES)
    column, lane = iota(shape, 0), iota(shape, 1)
    low = (column // GROUP) % DIGIT
    step = column // (GROUP * DIGIT)
    keep = low == lane % DIGIT
    if spread:
        keep = keep & (step == lane // BS)
    return keep.astype(F32).astype(BF16)


def fold_rows(wide):
    lane = iota((GROUP, LANES), 1) // DIGIT
    total = jnp.zeros((GROUP, LANES), F32)
    for s in range(NEWTON * DIGIT):
        total = total + jnp.where(lane == s, wide[s * GROUP : (s + 1) * GROUP], 0.0)
    return total


def split(value, parts):
    pieces = []
    for _ in range(parts):
        piece = value.astype(BF16)
        pieces.append(piece)
        value = value - piece.astype(F32)
    return pieces


def fields_of(table_ref):
    first = table_ref[0]
    return jnp.concatenate([first, first + table_ref[1]], axis=1)


def prepare_kernel(table_ref, send_ref):
    block_count = table_ref.shape[1]
    half = block_count // 2
    first = table_ref[0]
    packed = [
        jnp.concatenate([field[:half], field[half:]], axis=1).astype(BF16)
        for field in (first, first + table_ref[1])
    ]
    devices = send_ref.shape[0] // half
    for d in range(devices):
        send_ref[pl.ds(d * half, half), :] = packed[d * NEWTON // devices]


def inner_images(volt_rows, update_rows, cap_rows, source_ref, target_ref, gain_ref):
    block_count, elements = source_ref.shape
    nodes_any, nodes_step = gather_nodes(False), gather_nodes(True)
    images = []
    for start in range(0, block_count, GROUP):
        rows = slice(start, start + GROUP)
        volts, updates = volt_rows[rows], update_rows[rows]
        acc_ones = jnp.zeros((NEWTON * DIGIT * GROUP, DIGIT * GROUP), F32)
        acc = jnp.zeros((NEWTON * DIGIT * GROUP, NEWTON * DIGIT * GROUP), F32)
        for at in range(0, elements, LANES):
            lanes = slice(at, at + LANES)
            source, target = source_ref[rows, lanes], target_ref[rows, lanes]
            gain = jnp.where(source == target, 0.0, gain_ref[rows, lanes])
            weights, source_updates, target_updates = [], [], []
            for t in range(NEWTON):
                here, there = source + t * BS, target + t * BS
                weights.append(
                    conductance(gain, pick(volts, here), pick(volts, there)).astype(BF16)
                )
                source_updates.append(pick(updates, here).astype(BF16))
                target_updates.append(pick(updates, there).astype(BF16))
            ones = jnp.ones((GROUP, LANES), BF16)
            left, right, right_ones = [], [], []
            for index, others in ((source, target_updates), (target, source_updates)):
                high, low = digits(index)
                left.append(hot_rows(high, weights))
                right_ones.append(hot_rows(low, [ones]))
                right.append(hot_rows(low, others))
            left = jnp.concatenate(left, axis=1)
            acc_ones = acc_ones + dot(left, jnp.concatenate(right_ones, axis=1), NT)
            acc = acc + dot(left, jnp.concatenate(right, axis=1), NT)
        acc = jnp.where(same_block(acc.shape, GROUP), acc, 0.0)
        acc_ones = jnp.where(same_block(acc_ones.shape, GROUP), acc_ones, 0.0)
        diagonal = fold_rows(
            sum(dot(p, nodes_any[: DIGIT * GROUP], NN) for p in split(acc_ones, 2))
        )
        others = fold_rows(sum(dot(p, nodes_step, NN) for p in split(acc, 2)))
        diagonal = (diagonal + cap_rows[rows]).astype(BF16).astype(F32)
        images.append(diagonal * updates - others)
    return jnp.concatenate(images, axis=0)


def row_to_column(row):
    count = row.shape[1]
    shape = (count, count)
    return jnp.sum(jnp.where(iota(shape, 0) == iota(shape, 1), row, 0), axis=1, keepdims=True)


def inner_kernel(
    table_ref,
    cap_ref,
    inner_source_ref,
    inner_target_ref,
    inner_gain_ref,
    precond_ref,
    inner_ref,
    packed_ref,
):
    for g in range(packed_ref.shape[0]):
        parts = [precond_ref[i] for i in range(g, BS, packed_ref.shape[0])]
        packed_ref[g] = jnp.concatenate(parts, axis=0).T
    updates = jnp.concatenate([table_ref[1], table_ref[2]], axis=1).astype(BF16).astype(F32)
    caps = jnp.concatenate([cap_ref[...], cap_ref[...]], axis=1)
    inner_ref[...] = inner_images(
        fields_of(table_ref), updates, caps, inner_source_ref, inner_target_ref, inner_gain_ref
    ).T


def stamp_kernel(
    per_owner,
    facts_ref,
    facts_other,
    table_ref,
    table_other,
    source_ref,
    source_other,
    target_ref,
    target_other,
    gain_ref,
    gain_other,
    target_out,
    gain_out,
    near_ref,
    moved_ref,
    row_hot_ref,
    place_ref,
    offset_hot_ref,
):
    own_count, elements = source_ref.shape
    stamp_count = 2 * own_count
    block_count = table_ref.shape[1]
    half = block_count // 2
    later = lax.axis_index("sub") == 1
    tables = []
    for ref in (table_ref, table_other):
        field = jnp.where(later, ref[0] + ref[1], ref[0])
        update = jnp.where(later, ref[2], ref[1]).astype(BF16).astype(F32)
        tables.append(jnp.concatenate([field, update], axis=1))
    tables = jnp.concatenate(tables, axis=0)

    facts = jnp.concatenate([facts_ref[...], facts_other[...]], axis=1).astype(F32)
    block_row, owner_row, offset_row = facts[0:1], facts[1:2], facts[2:3]
    chip_row = jnp.floor(owner_row * 0.5)
    chips = row_hot_ref.shape[1] // (NEWTON * half)
    owner_row = (owner_row - NEWTON * chip_row) * chips + chip_row
    mine = iota((1, stamp_count), 1) < own_count
    block = row_to_column(jnp.where(mine, block_row, block_row + block_count))
    owner = row_to_column(owner_row)
    offset = row_to_column(offset_row)
    upper = jnp.where(offset < half, 0, 1)
    row_hot = iota(row_hot_ref.shape, 1).astype(F32) == owner * half + offset - half * upper.astype(F32)
    row_hot_ref[...] = row_hot.astype(F32).astype(BF16)
    shape = (stamp_count, stamp_count)
    row, column = iota(shape, 0), iota(shape, 1)
    earlier = (owner == owner_row) & (row < column) & ((row < own_count) == (column < own_count))
    rank_row = jnp.sum(jnp.where(earlier, 1.0, 0.0), axis=0, keepdims=True)
    rank_row = jnp.where(mine, rank_row, rank_row + per_owner)
    slot_row = owner_row * (2 * per_owner) + rank_row
    place = iota(place_ref.shape, 0).astype(F32) == slot_row
    place_ref[...] = place.astype(F32).astype(BF16)
    offset_hot = iota(offset_hot_ref.shape, 1).astype(F32) == offset
    offset_hot_ref[...] = offset_hot.astype(F32).astype(BF16)

    block_hot = iota((stamp_count, 2 * block_count), 1).astype(F32) == block
    block_hot = block_hot.astype(F32).astype(BF16)
    local = sum(dot(block_hot, p, NN) for p in split(tables, 3))
    for n, (sources, targets, gains) in enumerate(
        ((source_ref, target_ref, gain_ref), (source_other, target_other, gain_other))
    ):
        held = slice(n * own_count, (n + 1) * own_count)
        gain_out[held, :] = -gains[...]
        near = local[held]
        for at in range(0, elements, LANES):
            lanes = slice(at, at + LANES)
            source = sources[:, lanes]
            near_ref[held, lanes] = pick(near, source)
            moved_ref[held, lanes] = pick(near, source + BS).astype(BF16)
            target = targets[:, lanes] + upper[held] * BS
            target_out[held, lanes] = target.astype(F32).astype(BF16)

def couple_kernel(
    fields_ref,
    target_ref,
    gain_ref,
    near_ref,
    moved_ref,
    row_hot_ref,
    place_ref,
    offset_hot_ref,
    send_ref,
    product_ref,
):
    stamp_count, elements = target_ref.shape
    group = NEWTON * GROUP
    rows_of = DIGIT * group
    same = same_block((rows_of, rows_of), group)
    remote = dot(row_hot_ref[...], fields_ref[...], NN)
    for start in range(0, stamp_count, group):
        rows = slice(start, start + group)
        held = slice(DIGIT * start, DIGIT * start + rows_of)
        left, right = [], []
        for at in range(0, elements, LANES):
            lanes = slice(at, at + LANES)
            target = target_ref[rows, lanes].astype(F32).astype(jnp.int32)
            high, low = digits(target & (BS - 1))
            far = pick(remote[rows], target)
            weight = conductance(gain_ref[rows, lanes], near_ref[rows, lanes], far)
            left.append(hot_rows(high, [weight.astype(BF16)]))
            right.append(hot_rows(low, [moved_ref[rows, lanes]]))
        product = dot(jnp.concatenate(left, axis=1), jnp.concatenate(right, axis=1), NT)
        product_ref[held, :] = jnp.where(same, product, 0.0).astype(BF16)
    shape = (rows_of, LANES)
    node = iota(shape, 1) - BS
    nodes = (node >= 0) & (node % DIGIT == iota(shape, 0) // group)
    wide = dot(product_ref[...], nodes.astype(F32).astype(BF16), NN)
    high_lane = (iota((group, LANES), 1) - BS) // DIGIT
    images = []
    for start in range(0, DIGIT * stamp_count, rows_of):
        total = jnp.zeros((group, LANES), F32)
        for h in range(DIGIT):
            slab = wide[start + h * group : start + (h + 1) * group]
            total = total + jnp.where(high_lane == h, slab, 0.0)
        images.append(total)
    images = jnp.concatenate(images, axis=0)
    messages = images.astype(BF16) + offset_hot_ref[...]
    send_ref[...] = dot(place_ref[...], messages, NN).astype(BF16)


def finish_kernel(row_count, images_ref, inner_ref, packed_ref, out_ref):
    received = images_ref[...]
    block_count = inner_ref.shape[1]
    parts = LANES // block_count
    step = iota(received.shape, 0) // (received.shape[0] // NEWTON)
    totals = []
    for t in range(NEWTON):
        mine = jnp.where(step == t, received.astype(F32), 0.0).astype(BF16)
        couple = dot(received, mine, TN)[BS:, :block_count]
        total = inner_ref[t * BS : (t + 1) * BS, :] + couple
        totals.append(jnp.concatenate([total] * parts, axis=1))
    rows = [[] for _ in range(NEWTON)]
    for g in range(packed_ref.shape[0]):
        packed = packed_ref[g]
        for t in range(NEWTON):
            rows[t].append(jnp.sum(packed * totals[t], axis=0, keepdims=True))
    for t in range(NEWTON):
        wide = jnp.concatenate(rows[t], axis=0).T
        out_ref[t] = jnp.concatenate(
            [wide[k * block_count : (k + 1) * block_count] for k in range(parts)], axis=1
        )


def call(kernel, out_shape, args, cost, scratch=()):
    spec = pl.BlockSpec(memory_space=pltpu.VMEM)
    several = isinstance(out_shape, (list, tuple))
    return pl.pallas_call(
        kernel,
        out_shape=out_shape,
        in_specs=[spec] * len(args),
        out_specs=[spec] * len(out_shape) if several else spec,
        scratch_shapes=list(scratch),
        compiler_params=pltpu.CompilerParams(vmem_limit_bytes=24 * 2**20),
        cost_estimate=pl.CostEstimate(flops=cost[0], bytes_accessed=cost[1], transcendentals=0),
    )(*args)


def exchange(rows, devices):
    shaped = rows.reshape((devices, rows.shape[0] // devices, rows.shape[1]))
    out = lax.all_to_all(shaped, AXES[::-1], split_axis=0, concat_axis=0, tiled=True)
    return out.reshape(rows.shape)


def per_device(
    voltages,
    newton_steps,
    cap_diag,
    preconditioner,
    couple_block,
    couple_owner,
    couple_offset,
    couple_source,
    couple_target,
    couple_gain,
    inner_source,
    inner_target,
    inner_gain,
):
    devices = lax.axis_size(AXES)
    stamp_count, elements = couple_source.shape
    block_count = voltages.shape[1]
    per_owner = max(2, 2 * stamp_count // devices)
    row_count = devices * per_owner * NEWTON
    like = jax.ShapeDtypeStruct
    swap = lambda array: lax.ppermute(array, "sub", [(0, 1), (1, 0)])
    table = jnp.concatenate([voltages.T[None], newton_steps.transpose(0, 2, 1)], axis=0)
    send = call(
        prepare_kernel, like((devices * block_count // 2, LANES), BF16), (table,), (2 * 10**10, 10**6)
    )
    facts = [fact.reshape(1, stamp_count) for fact in (couple_block, couple_owner, couple_offset)]
    send, facts = lax.optimization_barrier((send, jnp.concatenate(facts, axis=0)))
    fields = exchange(send, devices)
    inner, packed = call(
        inner_kernel,
        [
            like((NEWTON * BS, block_count), F32),
            like((BS * block_count // LANES, BS, LANES), F32),
        ],
        (
            table,
            cap_diag.T,
            inner_source,
            inner_target,
            inner_gain,
            preconditioner.transpose(0, 2, 1),
        ),
        (10**9, 10**6),
    )
    wanted = (facts, table, couple_source, couple_target, couple_gain)
    pairs = [half for array in wanted for half in (array, swap(array))]
    both = 2 * stamp_count
    prepared = call(
        functools.partial(stamp_kernel, per_owner),
        [
            like((both, elements), BF16),
            like((both, elements), F32),
            like((both, elements), F32),
            like((both, elements), BF16),
            like((both, devices * block_count // 2), BF16),
            like((row_count, both), BF16),
            like((both, LANES), BF16),
        ],
        pairs,
        (10**8, 10**6),
    )
    fields, inner, packed = lax.optimization_barrier((fields, inner, packed))
    images = call(
        couple_kernel,
        like((row_count, LANES), BF16),
        (fields, *prepared),
        (4 * 10**9, 10**6),
        [
            pltpu.VMEM((DIGIT * both, DIGIT * NEWTON * GROUP), BF16),
        ],
    )
    received = exchange(images, devices)
    out = call(
        functools.partial(finish_kernel, 2 * per_owner),
        like((NEWTON, block_count, BS), F32),
        (received, inner, packed),
        (10**8, 10**6),
    )
    return out.transpose(0, 2, 1)


def solution(mesh):
    in_specs = (
        P(None, AXES),
        P(None, None, AXES),
        P(None, AXES),
        P(None, None, AXES),
        P(AXES),
        P(AXES, None),
        P(AXES),
        P(AXES, None),
        P(AXES, None),
        P(AXES, None),
        P(AXES, None),
        P(AXES, None),
        P(AXES, None),
    )
    out_specs = P(None, None, AXES)
    return jax.shard_map(
        per_device, mesh=mesh, in_specs=in_specs, out_specs=out_specs, check_vma=False
    )
```

```python
import functools

import jax
import jax.numpy as jnp
from jax import lax
from jax.experimental import pallas as pl
from jax.experimental.pallas import tpu as pltpu
from jax.sharding import PartitionSpec as P

BS = 64
NEWTON = 2
LANES = 128
GROUP = 16
DIGIT = 8
AXES = ("dom", "sub")
NT = (((1,), (1,)), ((), ()))
TN = (((0,), (0,)), ((), ()))
NN = (((1,), (0,)), ((), ()))
F32 = jnp.float32
BF16 = jnp.bfloat16


def iota(shape, axis):
    return lax.broadcasted_iota(jnp.int32, shape, axis)


def dot(first, second, numbers):
    return lax.dot_general(first, second, numbers, preferred_element_type=F32)


def pick(table, index):
    return jnp.concatenate(
        [
            jnp.take_along_axis(table[r : r + 8], index[r : r + 8], axis=1)
            for r in range(0, table.shape[0], 8)
        ],
        axis=0,
    )


def conductance(gain, first, second):
    drop = first - second
    return gain / (1.0 + drop * drop)


def digits(index):
    high = lax.shift_right_logical(index, 3)
    return high.astype(F32).astype(BF16), (index - high * DIGIT).astype(F32).astype(BF16)


def hot_rows(digit, values):
    zero = jnp.zeros_like(values[0])
    masks = [digit == jnp.asarray(d, BF16) for d in range(DIGIT)]
    return jnp.concatenate([jnp.where(m, v, zero) for v in values for m in masks], axis=0)


def same_block(shape, group):
    return (iota(shape, 0) % group) == (iota(shape, 1) % group)


def gather_nodes(spread):
    shape = (NEWTON * DIGIT * GROUP, LANES)
    column, lane = iota(shape, 0), iota(shape, 1)
    low = (column // GROUP) % DIGIT
    step = column // (GROUP * DIGIT)
    keep = low == lane % DIGIT
    if spread:
        keep = keep & (step == lane // BS)
    return keep.astype(F32).astype(BF16)


def fold_rows(wide):
    lane = iota((GROUP, LANES), 1) // DIGIT
    total = jnp.zeros((GROUP, LANES), F32)
    for s in range(NEWTON * DIGIT):
        total = total + jnp.where(lane == s, wide[s * GROUP : (s + 1) * GROUP], 0.0)
    return total


def split(value, parts):
    pieces = []
    for _ in range(parts):
        piece = value.astype(BF16)
        pieces.append(piece)
        value = value - piece.astype(F32)
    return pieces


def fields_of(table_ref):
    first = table_ref[0]
    return jnp.concatenate([first, first + table_ref[1]], axis=1)


def prepare_kernel(volt_ref, step_ref, send_ref):
    block_count = volt_ref.shape[0]
    half = block_count // 2
    first = volt_ref[...]
    packed = [
        jnp.concatenate([field[:half], field[half:]], axis=1).astype(BF16)
        for field in (first, first + step_ref[...])
    ]
    devices = send_ref.shape[0] // half
    for d in range(devices):
        send_ref[pl.ds(d * half, half), :] = packed[d * NEWTON // devices]


def inner_images(volt_rows, update_rows, cap_rows, source_ref, target_ref, gain_ref):
    block_count, elements = source_ref.shape
    nodes_any, nodes_step = gather_nodes(False), gather_nodes(True)
    images = []
    for start in range(0, block_count, GROUP):
        rows = slice(start, start + GROUP)
        volts, updates = volt_rows[rows], update_rows[rows]
        acc_ones = jnp.zeros((NEWTON * DIGIT * GROUP, DIGIT * GROUP), F32)
        acc = jnp.zeros((NEWTON * DIGIT * GROUP, NEWTON * DIGIT * GROUP), F32)
        for at in range(0, elements, LANES):
            lanes = slice(at, at + LANES)
            source, target = source_ref[rows, lanes], target_ref[rows, lanes]
            gain = jnp.where(source == target, 0.0, gain_ref[rows, lanes])
            weights, source_updates, target_updates = [], [], []
            for t in range(NEWTON):
                here, there = source + t * BS, target + t * BS
                weights.append(
                    conductance(gain, pick(volts, here), pick(volts, there)).astype(BF16)
                )
                source_updates.append(pick(updates, here).astype(BF16))
                target_updates.append(pick(updates, there).astype(BF16))
            ones = jnp.ones((GROUP, LANES), BF16)
            left, right, right_ones = [], [], []
            for index, others in ((source, target_updates), (target, source_updates)):
                high, low = digits(index)
                left.append(hot_rows(high, weights))
                right_ones.append(hot_rows(low, [ones]))
                right.append(hot_rows(low, others))
            left = jnp.concatenate(left, axis=1)
            acc_ones = acc_ones + dot(left, jnp.concatenate(right_ones, axis=1), NT)
            acc = acc + dot(left, jnp.concatenate(right, axis=1), NT)
        acc = jnp.where(same_block(acc.shape, GROUP), acc, 0.0)
        acc_ones = jnp.where(same_block(acc_ones.shape, GROUP), acc_ones, 0.0)
        diagonal = fold_rows(
            sum(dot(p, nodes_any[: DIGIT * GROUP], NN) for p in split(acc_ones, 2))
        )
        others = fold_rows(sum(dot(p, nodes_step, NN) for p in split(acc, 2)))
        diagonal = (diagonal + cap_rows[rows]).astype(BF16).astype(F32)
        images.append(diagonal * updates - others)
    return jnp.concatenate(images, axis=0)


def row_to_column(row):
    count = row.shape[1]
    shape = (count, count)
    return jnp.sum(jnp.where(iota(shape, 0) == iota(shape, 1), row, 0), axis=1, keepdims=True)


def inner_kernel(
    table_ref,
    cap_ref,
    inner_source_ref,
    inner_target_ref,
    inner_gain_ref,
    precond_ref,
    inner_ref,
    packed_ref,
):
    for g in range(packed_ref.shape[0]):
        parts = [precond_ref[i] for i in range(g, BS, packed_ref.shape[0])]
        packed_ref[g] = jnp.concatenate(parts, axis=0).T
    updates = jnp.concatenate([table_ref[1], table_ref[2]], axis=1).astype(BF16).astype(F32)
    caps = jnp.concatenate([cap_ref[...], cap_ref[...]], axis=1)
    inner_ref[...] = inner_images(
        fields_of(table_ref), updates, caps, inner_source_ref, inner_target_ref, inner_gain_ref
    ).T


def stamp_kernel(
    per_owner,
    facts_ref,
    facts_other,
    table_ref,
    table_other,
    source_ref,
    source_other,
    target_ref,
    target_other,
    gain_ref,
    gain_other,
    target_out,
    gain_out,
    near_ref,
    moved_ref,
    row_hot_ref,
    place_ref,
    offset_hot_ref,
):
    own_count, elements = source_ref.shape
    stamp_count = 2 * own_count
    block_count = table_ref.shape[1]
    half = block_count // 2
    later = lax.axis_index("sub") == 1
    tables = []
    for ref in (table_ref, table_other):
        field = jnp.where(later, ref[0] + ref[1], ref[0])
        update = jnp.where(later, ref[2], ref[1]).astype(BF16).astype(F32)
        tables.append(jnp.concatenate([field, update], axis=1))
    tables = jnp.concatenate(tables, axis=0)

    facts = jnp.concatenate([facts_ref[...], facts_other[...]], axis=1).astype(F32)
    block_row, owner_row, offset_row = facts[0:1], facts[1:2], facts[2:3]
    chip_row = jnp.floor(owner_row * 0.5)
    chips = row_hot_ref.shape[1] // (NEWTON * half)
    owner_row = (owner_row - NEWTON * chip_row) * chips + chip_row
    mine = iota((1, stamp_count), 1) < own_count
    block = row_to_column(jnp.where(mine, block_row, block_row + block_count))
    owner = row_to_column(owner_row)
    offset = row_to_column(offset_row)
    upper = jnp.where(offset < half, 0, 1)
    row_hot = iota(row_hot_ref.shape, 1).astype(F32) == owner * half + offset - half * upper.astype(F32)
    row_hot_ref[...] = row_hot.astype(F32).astype(BF16)
    shape = (stamp_count, stamp_count)
    row, column = iota(shape, 0), iota(shape, 1)
    earlier = (owner == owner_row) & (row < column) & ((row < own_count) == (column < own_count))
    rank_row = jnp.sum(jnp.where(earlier, 1.0, 0.0), axis=0, keepdims=True)
    rank_row = jnp.where(mine, rank_row, rank_row + per_owner)
    slot_row = owner_row * (2 * per_owner) + rank_row
    place = iota(place_ref.shape, 0).astype(F32) == slot_row
    place_ref[...] = place.astype(F32).astype(BF16)
    offset_hot = iota(offset_hot_ref.shape, 1).astype(F32) == offset
    offset_hot_ref[...] = offset_hot.astype(F32).astype(BF16)

    block_hot = iota((stamp_count, 2 * block_count), 1).astype(F32) == block
    block_hot = block_hot.astype(F32).astype(BF16)
    local = sum(dot(block_hot, p, NN) for p in split(tables, 3))
    for n, (sources, targets, gains) in enumerate(
        ((source_ref, target_ref, gain_ref), (source_other, target_other, gain_other))
    ):
        held = slice(n * own_count, (n + 1) * own_count)
        gain_out[held, :] = (-gains[...]).astype(BF16)
        near = local[held]
        for at in range(0, elements, LANES):
            lanes = slice(at, at + LANES)
            source = sources[:, lanes]
            near_ref[held, lanes] = pick(near, source).astype(BF16)
            moved_ref[held, lanes] = pick(near, source + BS).astype(BF16)
            target = targets[:, lanes] + upper[held] * BS
            target_out[held, lanes] = target.astype(F32).astype(BF16)

def couple_kernel(
    fields_ref,
    target_ref,
    gain_ref,
    near_ref,
    moved_ref,
    row_hot_ref,
    place_ref,
    offset_hot_ref,
    send_ref,
    product_ref,
):
    stamp_count, elements = target_ref.shape
    group = NEWTON * GROUP
    rows_of = DIGIT * group
    same = same_block((rows_of, rows_of), group)
    remote = dot(row_hot_ref[...], fields_ref[...], NN)
    for start in range(0, stamp_count, group):
        rows = slice(start, start + group)
        held = slice(DIGIT * start, DIGIT * start + rows_of)
        left, right = [], []
        for at in range(0, elements, LANES):
            lanes = slice(at, at + LANES)
            target = target_ref[rows, lanes].astype(F32).astype(jnp.int32)
            high, low = digits(target & (BS - 1))
            far = pick(remote[rows], target)
            gain, near = gain_ref[rows, lanes].astype(F32), near_ref[rows, lanes].astype(F32)
            weight = conductance(gain, near, far)
            left.append(hot_rows(high, [weight.astype(BF16)]))
            right.append(hot_rows(low, [moved_ref[rows, lanes]]))
        product = dot(jnp.concatenate(left, axis=1), jnp.concatenate(right, axis=1), NT)
        product_ref[held, :] = jnp.where(same, product, 0.0).astype(BF16)
    shape = (rows_of, LANES)
    node = iota(shape, 1) - BS
    nodes = (node >= 0) & (node % DIGIT == iota(shape, 0) // group)
    wide = dot(product_ref[...], nodes.astype(F32).astype(BF16), NN)
    high_lane = (iota((group, LANES), 1) - BS) // DIGIT
    images = []
    for start in range(0, DIGIT * stamp_count, rows_of):
        total = jnp.zeros((group, LANES), F32)
        for h in range(DIGIT):
            slab = wide[start + h * group : start + (h + 1) * group]
            total = total + jnp.where(high_lane == h, slab, 0.0)
        images.append(total)
    images = jnp.concatenate(images, axis=0)
    messages = images.astype(BF16) + offset_hot_ref[...]
    send_ref[...] = dot(place_ref[...], messages, NN).astype(BF16)


def finish_kernel(row_count, images_ref, inner_ref, packed_ref, out_ref):
    received = images_ref[...]
    block_count = inner_ref.shape[1]
    parts = LANES // block_count
    step = iota(received.shape, 0) // (received.shape[0] // NEWTON)
    totals = []
    for t in range(NEWTON):
        mine = jnp.where(step == t, received.astype(F32), 0.0).astype(BF16)
        couple = dot(received, mine, TN)[BS:, :block_count]
        total = inner_ref[t * BS : (t + 1) * BS, :] + couple
        totals.append(jnp.concatenate([total] * parts, axis=1))
    rows = [[] for _ in range(NEWTON)]
    for g in range(packed_ref.shape[0]):
        packed = packed_ref[g]
        for t in range(NEWTON):
            rows[t].append(jnp.sum(packed * totals[t], axis=0, keepdims=True))
    for t in range(NEWTON):
        wide = jnp.concatenate(rows[t], axis=0).T
        out_ref[t] = jnp.concatenate(
            [wide[k * block_count : (k + 1) * block_count] for k in range(parts)], axis=1
        )


def call(kernel, out_shape, args, cost, scratch=()):
    spec = pl.BlockSpec(memory_space=pltpu.VMEM)
    several = isinstance(out_shape, (list, tuple))
    return pl.pallas_call(
        kernel,
        out_shape=out_shape,
        in_specs=[spec] * len(args),
        out_specs=[spec] * len(out_shape) if several else spec,
        scratch_shapes=list(scratch),
        compiler_params=pltpu.CompilerParams(vmem_limit_bytes=24 * 2**20),
        cost_estimate=pl.CostEstimate(flops=cost[0], bytes_accessed=cost[1], transcendentals=0),
    )(*args)


def exchange(rows, devices):
    shaped = rows.reshape((devices, rows.shape[0] // devices, rows.shape[1]))
    out = lax.all_to_all(shaped, AXES[::-1], split_axis=0, concat_axis=0, tiled=True)
    return out.reshape(rows.shape)


def per_device(
    voltages,
    newton_steps,
    cap_diag,
    preconditioner,
    couple_block,
    couple_owner,
    couple_offset,
    couple_source,
    couple_target,
    couple_gain,
    inner_source,
    inner_target,
    inner_gain,
):
    devices = lax.axis_size(AXES)
    stamp_count, elements = couple_source.shape
    block_count = voltages.shape[1]
    per_owner = max(2, 2 * stamp_count // devices)
    row_count = devices * per_owner * NEWTON
    like = jax.ShapeDtypeStruct
    swap = lambda array: lax.ppermute(array, "sub", [(0, 1), (1, 0)])
    table = jnp.concatenate([voltages.T[None], newton_steps.transpose(0, 2, 1)], axis=0)
    send = call(
        prepare_kernel, like((devices * block_count // 2, LANES), BF16), (voltages.T, newton_steps[0].T), (2 * 10**10, 10**6)
    )
    facts = [fact.reshape(1, stamp_count) for fact in (couple_block, couple_owner, couple_offset)]
    send, facts = lax.optimization_barrier((send, jnp.concatenate(facts, axis=0)))
    fields = exchange(send, devices)
    inner, packed = call(
        inner_kernel,
        [
            like((NEWTON * BS, block_count), F32),
            like((BS * block_count // LANES, BS, LANES), F32),
        ],
        (
            table,
            cap_diag.T,
            inner_source,
            inner_target,
            inner_gain,
            preconditioner.transpose(0, 2, 1),
        ),
        (10**9, 10**6),
    )
    wanted = (facts, table, couple_source, couple_target, couple_gain)
    pairs = [half for array in wanted for half in (array, swap(array))]
    both = 2 * stamp_count
    prepared = call(
        functools.partial(stamp_kernel, per_owner),
        [
            like((both, elements), BF16),
            like((both, elements), BF16),
            like((both, elements), BF16),
            like((both, elements), BF16),
            like((both, devices * block_count // 2), BF16),
            like((row_count, both), BF16),
            like((both, LANES), BF16),
        ],
        pairs,
        (10**8, 10**6),
    )
    fields, inner, packed = lax.optimization_barrier((fields, inner, packed))
    images = call(
        couple_kernel,
        like((row_count, LANES), BF16),
        (fields, *prepared),
        (4 * 10**9, 10**6),
        [
            pltpu.VMEM((DIGIT * both, DIGIT * NEWTON * GROUP), BF16),
        ],
    )
    received = exchange(images, devices)
    out = call(
        functools.partial(finish_kernel, 2 * per_owner),
        like((NEWTON, block_count, BS), F32),
        (received, inner, packed),
        (10**8, 10**6),
    )
    return out.transpose(0, 2, 1)


def solution(mesh):
    in_specs = (
        P(None, AXES),
        P(None, None, AXES),
        P(None, AXES),
        P(None, None, AXES),
        P(AXES),
        P(AXES, None),
        P(AXES),
        P(AXES, None),
        P(AXES, None),
        P(AXES, None),
        P(AXES, None),
        P(AXES, None),
        P(AXES, None),
    )
    out_specs = P(None, None, AXES)
    return jax.shard_map(
        per_device, mesh=mesh, in_specs=in_specs, out_specs=out_specs, check_vma=False
    )
```

```python
import functools

import jax
import jax.numpy as jnp
from jax import lax
from jax.experimental import pallas as pl
from jax.experimental.pallas import tpu as pltpu
from jax.sharding import PartitionSpec as P

BS = 64
NEWTON = 2
LANES = 128
GROUP = 16
DIGIT = 8
AXES = ("dom", "sub")
NT = (((1,), (1,)), ((), ()))
TN = (((0,), (0,)), ((), ()))
NN = (((1,), (0,)), ((), ()))
F32 = jnp.float32
BF16 = jnp.bfloat16


def iota(shape, axis):
    return lax.broadcasted_iota(jnp.int32, shape, axis)


def dot(first, second, numbers):
    return lax.dot_general(first, second, numbers, preferred_element_type=F32)


def pick(table, index):
    return jnp.concatenate(
        [
            jnp.take_along_axis(table[r : r + 8], index[r : r + 8], axis=1)
            for r in range(0, table.shape[0], 8)
        ],
        axis=0,
    )


def conductance(gain, first, second):
    drop = first - second
    return gain / (1.0 + drop * drop)


def digits(index):
    high = lax.shift_right_logical(index, 3)
    return high.astype(F32).astype(BF16), (index - high * DIGIT).astype(F32).astype(BF16)


def hot_rows(digit, values):
    zero = jnp.zeros_like(values[0])
    masks = [digit == jnp.asarray(d, BF16) for d in range(DIGIT)]
    return jnp.concatenate([jnp.where(m, v, zero) for v in values for m in masks], axis=0)


def same_block(shape, group):
    return (iota(shape, 0) % group) == (iota(shape, 1) % group)


def gather_nodes(spread):
    shape = (NEWTON * DIGIT * GROUP, LANES)
    column, lane = iota(shape, 0), iota(shape, 1)
    low = (column // GROUP) % DIGIT
    step = column // (GROUP * DIGIT)
    keep = low == lane % DIGIT
    if spread:
        keep = keep & (step == lane // BS)
    return keep.astype(F32).astype(BF16)


def fold_rows(wide):
    lane = iota((GROUP, LANES), 1) // DIGIT
    total = jnp.zeros((GROUP, LANES), F32)
    for s in range(NEWTON * DIGIT):
        total = total + jnp.where(lane == s, wide[s * GROUP : (s + 1) * GROUP], 0.0)
    return total


def split(value, parts):
    pieces = []
    for _ in range(parts):
        piece = value.astype(BF16)
        pieces.append(piece)
        value = value - piece.astype(F32)
    return pieces


def fields_of(table_ref):
    first = table_ref[0]
    return jnp.concatenate([first, first + table_ref[1]], axis=1)


def prepare_kernel(table_ref, send_ref):
    block_count = table_ref.shape[1]
    half = block_count // 2
    first = table_ref[0]
    packed = [
        jnp.concatenate([field[:half], field[half:]], axis=1).astype(BF16)
        for field in (first, first + table_ref[1])
    ]
    devices = send_ref.shape[0] // half
    for d in range(devices):
        send_ref[pl.ds(d * half, half), :] = packed[d * NEWTON // devices]


def inner_images(volt_rows, update_rows, cap_rows, source_ref, target_ref, gain_ref):
    block_count, elements = source_ref.shape
    nodes_any, nodes_step = gather_nodes(False), gather_nodes(True)
    images = []
    for start in range(0, block_count, GROUP):
        rows = slice(start, start + GROUP)
        volts, updates = volt_rows[rows], update_rows[rows]
        acc_ones = jnp.zeros((NEWTON * DIGIT * GROUP, DIGIT * GROUP), F32)
        acc = jnp.zeros((NEWTON * DIGIT * GROUP, NEWTON * DIGIT * GROUP), F32)
        for at in range(0, elements, LANES):
            lanes = slice(at, at + LANES)
            source, target = source_ref[rows, lanes], target_ref[rows, lanes]
            gain = jnp.where(source == target, 0.0, gain_ref[rows, lanes])
            weights, source_updates, target_updates = [], [], []
            for t in range(NEWTON):
                here, there = source + t * BS, target + t * BS
                weights.append(
                    conductance(gain, pick(volts, here), pick(volts, there)).astype(BF16)
                )
                source_updates.append(pick(updates, here).astype(BF16))
                target_updates.append(pick(updates, there).astype(BF16))
            ones = jnp.ones((GROUP, LANES), BF16)
            left, right, right_ones = [], [], []
            for index, others in ((source, target_updates), (target, source_updates)):
                high, low = digits(index)
                left.append(hot_rows(high, weights))
                right_ones.append(hot_rows(low, [ones]))
                right.append(hot_rows(low, others))
            left = jnp.concatenate(left, axis=1)
            acc_ones = acc_ones + dot(left, jnp.concatenate(right_ones, axis=1), NT)
            acc = acc + dot(left, jnp.concatenate(right, axis=1), NT)
        acc = jnp.where(same_block(acc.shape, GROUP), acc, 0.0)
        acc_ones = jnp.where(same_block(acc_ones.shape, GROUP), acc_ones, 0.0)
        diagonal = fold_rows(
            sum(dot(p, nodes_any[: DIGIT * GROUP], NN) for p in split(acc_ones, 2))
        )
        others = fold_rows(sum(dot(p, nodes_step, NN) for p in split(acc, 2)))
        diagonal = (diagonal + cap_rows[rows]).astype(BF16).astype(F32)
        images.append(diagonal * updates - others)
    return jnp.concatenate(images, axis=0)


def row_to_column(row):
    count = row.shape[1]
    shape = (count, count)
    return jnp.sum(jnp.where(iota(shape, 0) == iota(shape, 1), row, 0), axis=1, keepdims=True)


def inner_kernel(
    table_ref,
    cap_ref,
    inner_source_ref,
    inner_target_ref,
    inner_gain_ref,
    precond_ref,
    inner_ref,
    packed_ref,
):
    for g in range(packed_ref.shape[0]):
        parts = [precond_ref[i] for i in range(g, BS, packed_ref.shape[0])]
        packed_ref[g] = jnp.concatenate(parts, axis=0).T
    updates = jnp.concatenate([table_ref[1], table_ref[2]], axis=1).astype(BF16).astype(F32)
    caps = jnp.concatenate([cap_ref[...], cap_ref[...]], axis=1)
    inner_ref[...] = inner_images(
        fields_of(table_ref), updates, caps, inner_source_ref, inner_target_ref, inner_gain_ref
    ).T


def stamp_kernel(
    per_owner,
    facts_ref,
    facts_other,
    table_ref,
    table_other,
    source_ref,
    source_other,
    target_ref,
    target_other,
    gain_ref,
    gain_other,
    target_out,
    gain_out,
    near_ref,
    moved_ref,
    row_hot_ref,
    place_ref,
    offset_hot_ref,
):
    own_count, elements = source_ref.shape
    stamp_count = 2 * own_count
    block_count = table_ref.shape[1]
    half = block_count // 2
    later = lax.axis_index("sub") == 1
    tables = []
    for ref in (table_ref, table_other):
        field = jnp.where(later, ref[0] + ref[1], ref[0])
        update = jnp.where(later, ref[2], ref[1]).astype(BF16).astype(F32)
        tables.append(jnp.concatenate([field, update], axis=1))
    tables = jnp.concatenate(tables, axis=0)

    facts = jnp.concatenate([facts_ref[...], facts_other[...]], axis=1).astype(F32)
    block_row, owner_row, offset_row = facts[0:1], facts[1:2], facts[2:3]
    chip_row = jnp.floor(owner_row * 0.5)
    chips = row_hot_ref.shape[1] // (NEWTON * half)
    owner_row = (owner_row - NEWTON * chip_row) * chips + chip_row
    mine = iota((1, stamp_count), 1) < own_count
    block = row_to_column(jnp.where(mine, block_row, block_row + block_count))
    owner = row_to_column(owner_row)
    offset = row_to_column(offset_row)
    upper = jnp.where(offset < half, 0, 1)
    row_hot = iota(row_hot_ref.shape, 1).astype(F32) == owner * half + offset - half * upper.astype(F32)
    row_hot_ref[...] = row_hot.astype(F32).astype(BF16)
    shape = (stamp_count, stamp_count)
    row, column = iota(shape, 0), iota(shape, 1)
    earlier = (owner == owner_row) & (row < column) & ((row < own_count) == (column < own_count))
    rank_row = jnp.sum(jnp.where(earlier, 1.0, 0.0), axis=0, keepdims=True)
    rank_row = jnp.where(mine, rank_row, rank_row + per_owner)
    slot_row = owner_row * (2 * per_owner) + rank_row
    place = iota(place_ref.shape, 0).astype(F32) == slot_row
    place_ref[...] = place.astype(F32).astype(BF16)
    offset_hot = iota(offset_hot_ref.shape, 1).astype(F32) == offset
    offset_hot_ref[...] = offset_hot.astype(F32).astype(BF16)

    block_hot = iota((stamp_count, 2 * block_count), 1).astype(F32) == block
    block_hot = block_hot.astype(F32).astype(BF16)
    local = sum(dot(block_hot, p, NN) for p in split(tables, 3))
    for n, (sources, targets, gains) in enumerate(
        ((source_ref, target_ref, gain_ref), (source_other, target_other, gain_other))
    ):
        held = slice(n * own_count, (n + 1) * own_count)
        gain_out[held, :] = -gains[...]
        near = local[held]
        for at in range(0, elements, LANES):
            lanes = slice(at, at + LANES)
            source = sources[:, lanes]
            near_ref[held, lanes] = pick(near, source)
            moved_ref[held, lanes] = pick(near, source + BS).astype(BF16)
            target = targets[:, lanes] + upper[held] * BS
            target_out[held, lanes] = target.astype(F32).astype(BF16)

def couple_kernel(
    fields_ref,
    target_ref,
    gain_ref,
    near_ref,
    moved_ref,
    row_hot_ref,
    place_ref,
    offset_hot_ref,
    send_ref,
    product_ref,
):
    stamp_count, elements = target_ref.shape
    group = NEWTON * GROUP
    rows_of = DIGIT * group
    same = same_block((rows_of, rows_of), group)
    remote = dot(row_hot_ref[...], fields_ref[...], NN)
    for start in range(0, stamp_count, group):
        rows = slice(start, start + group)
        held = slice(DIGIT * start, DIGIT * start + rows_of)
        left, right = [], []
        for at in range(0, elements, LANES):
            lanes = slice(at, at + LANES)
            target = target_ref[rows, lanes].astype(F32).astype(jnp.int32)
            high, low = digits(target & (BS - 1))
            far = pick(remote[rows], target)
            weight = conductance(gain_ref[rows, lanes], near_ref[rows, lanes], far)
            left.append(hot_rows(high, [weight.astype(BF16)]))
            right.append(hot_rows(low, [moved_ref[rows, lanes]]))
        product = dot(jnp.concatenate(left, axis=1), jnp.concatenate(right, axis=1), NT)
        product_ref[held, :] = jnp.where(same, product.astype(BF16), jnp.zeros((), BF16))
    shape = (rows_of, LANES)
    node = iota(shape, 1) - BS
    nodes = (node >= 0) & (node % DIGIT == iota(shape, 0) // group)
    wide = dot(product_ref[...], nodes.astype(F32).astype(BF16), NN)
    high_lane = (iota((group, LANES), 1) - BS) // DIGIT
    images = []
    for start in range(0, DIGIT * stamp_count, rows_of):
        total = jnp.zeros((group, LANES), F32)
        for h in range(DIGIT):
            slab = wide[start + h * group : start + (h + 1) * group]
            total = total + jnp.where(high_lane == h, slab, 0.0)
        images.append(total)
    images = jnp.concatenate(images, axis=0)
    messages = images.astype(BF16) + offset_hot_ref[...]
    send_ref[...] = dot(place_ref[...], messages, NN).astype(BF16)


def finish_kernel(row_count, images_ref, inner_ref, packed_ref, out_ref):
    received = images_ref[...]
    block_count = inner_ref.shape[1]
    parts = LANES // block_count
    step = iota(received.shape, 0) // (received.shape[0] // NEWTON)
    totals = []
    for t in range(NEWTON):
        mine = jnp.where(step == t, received, jnp.zeros((), BF16))
        couple = dot(received, mine, TN)[BS:, :block_count]
        total = inner_ref[t * BS : (t + 1) * BS, :] + couple
        totals.append(jnp.concatenate([total] * parts, axis=1))
    rows = [[] for _ in range(NEWTON)]
    for g in range(packed_ref.shape[0]):
        packed = packed_ref[g]
        for t in range(NEWTON):
            rows[t].append(jnp.sum(packed * totals[t], axis=0, keepdims=True))
    for t in range(NEWTON):
        wide = jnp.concatenate(rows[t], axis=0).T
        out_ref[t] = jnp.concatenate(
            [wide[k * block_count : (k + 1) * block_count] for k in range(parts)], axis=1
        )


def call(kernel, out_shape, args, cost, scratch=()):
    spec = pl.BlockSpec(memory_space=pltpu.VMEM)
    several = isinstance(out_shape, (list, tuple))
    return pl.pallas_call(
        kernel,
        out_shape=out_shape,
        in_specs=[spec] * len(args),
        out_specs=[spec] * len(out_shape) if several else spec,
        scratch_shapes=list(scratch),
        compiler_params=pltpu.CompilerParams(vmem_limit_bytes=24 * 2**20),
        cost_estimate=pl.CostEstimate(flops=cost[0], bytes_accessed=cost[1], transcendentals=0),
    )(*args)


def exchange(rows, devices):
    shaped = rows.reshape((devices, rows.shape[0] // devices, rows.shape[1]))
    out = lax.all_to_all(shaped, AXES[::-1], split_axis=0, concat_axis=0, tiled=True)
    return out.reshape(rows.shape)


def per_device(
    voltages,
    newton_steps,
    cap_diag,
    preconditioner,
    couple_block,
    couple_owner,
    couple_offset,
    couple_source,
    couple_target,
    couple_gain,
    inner_source,
    inner_target,
    inner_gain,
):
    devices = lax.axis_size(AXES)
    stamp_count, elements = couple_source.shape
    block_count = voltages.shape[1]
    per_owner = max(2, 2 * stamp_count // devices)
    row_count = devices * per_owner * NEWTON
    like = jax.ShapeDtypeStruct
    swap = lambda array: lax.ppermute(array, "sub", [(0, 1), (1, 0)])
    table = jnp.concatenate([voltages.T[None], newton_steps.transpose(0, 2, 1)], axis=0)
    send = call(
        prepare_kernel, like((devices * block_count // 2, LANES), BF16), (table,), (2 * 10**10, 10**6)
    )
    facts = [fact.reshape(1, stamp_count) for fact in (couple_block, couple_owner, couple_offset)]
    send, facts = lax.optimization_barrier((send, jnp.concatenate(facts, axis=0)))
    fields = exchange(send, devices)
    inner, packed = call(
        inner_kernel,
        [
            like((NEWTON * BS, block_count), F32),
            like((BS * block_count // LANES, BS, LANES), F32),
        ],
        (
            table,
            cap_diag.T,
            inner_source,
            inner_target,
            inner_gain,
            preconditioner.transpose(0, 2, 1),
        ),
        (10**9, 10**6),
    )
    wanted = (facts, table, couple_source, couple_target, couple_gain)
    pairs = [half for array in wanted for half in (array, swap(array))]
    both = 2 * stamp_count
    prepared = call(
        functools.partial(stamp_kernel, per_owner),
        [
            like((both, elements), BF16),
            like((both, elements), F32),
            like((both, elements), F32),
            like((both, elements), BF16),
            like((both, devices * block_count // 2), BF16),
            like((row_count, both), BF16),
            like((both, LANES), BF16),
        ],
        pairs,
        (10**8, 10**6),
    )
    fields, inner, packed = lax.optimization_barrier((fields, inner, packed))
    images = call(
        couple_kernel,
        like((row_count, LANES), BF16),
        (fields, *prepared),
        (4 * 10**9, 10**6),
        [
            pltpu.VMEM((DIGIT * both, DIGIT * NEWTON * GROUP), BF16),
        ],
    )
    received = exchange(images, devices)
    out = call(
        functools.partial(finish_kernel, 2 * per_owner),
        like((NEWTON, block_count, BS), F32),
        (received, inner, packed),
        (10**8, 10**6),
    )
    return out.transpose(0, 2, 1)


def solution(mesh):
    in_specs = (
        P(None, AXES),
        P(None, None, AXES),
        P(None, AXES),
        P(None, None, AXES),
        P(AXES),
        P(AXES, None),
        P(AXES),
        P(AXES, None),
        P(AXES, None),
        P(AXES, None),
        P(AXES, None),
        P(AXES, None),
        P(AXES, None),
    )
    out_specs = P(None, None, AXES)
    return jax.shard_map(
        per_device, mesh=mesh, in_specs=in_specs, out_specs=out_specs, check_vma=False
    )
```
